32 devices in a mesh: dp: 4 (over y, x), expert: 4 (over z), tensor: 2 (over core).
Axes of the slice: x: 2, y: 2, z: 4, core: 2. Of those that a mesh axis runs over, the one named last changes fastest.
Arguments:
- tokens: bfloat16 [192, 3072], P('expert', 'tensor'), may hold values from -6 to 6
- cotangent: bfloat16 [192, 3072], P('expert', 'tensor'), may hold values from -6 to 6
- expert_ids: int32 [192, 2], P('expert'), may hold values from 0 to 3, all different within a row; in each aligned block of 48 rows (0 to 47, 48 to 95, ...) at most 32 rows name the same one
- gate_probs: bfloat16 [192, 2], P('expert'), may hold values from 0.049804688 to 0.94921875
- tenant_ids: int32 [192], P('expert'), may hold values from 0 to 7
- w_gate: bfloat16 [4, 3072, 1024], P('expert', None, ('dp', 'tensor')), may hold values from -0.109375 to 0.109375
- w_up: bfloat16 [4, 3072, 1024], P('expert', None, ('dp', 'tensor')), may hold values from -0.109375 to 0.109375
- w_down: bfloat16 [4, 1024, 3072], P('expert', ('dp', 'tensor')), may hold values from -0.1875 to 0.1875
- adapter_in: bfloat16 [4, 1024, 128], P('expert', ('dp', 'tensor')), may hold values from -0.1875 to 0.1875
- adapter_out: bfloat16 [4, 128, 3072], P('expert'), may hold values from -0.109375 to 0.109375
Outputs:
- input_grad: bfloat16 [192, 3072], P('expert', ('dp', 'tensor'))
- grad_in: float32 [4, 1024, 128], P('expert', ('dp', 'tensor'))
- grad_out: float32 [4, 128, 3072], P('expert', None, 'tensor')
The draws below stay inside these ranges and needn't reach their ends.
Inputs may be any that keep to these rules, and one draw needn't show every extreme that they name: `expert_ids`: the two experts of a token differ. Among the 48 tokens of each group (aligned blocks of the token rows of one index of expert), no expert is named more than 32 times, and in every draw some expert is named exactly 32 times in some group.
All inputs are finite; a program needn't handle non-finite values.
Results may differ from the reference program's by a relative error of at most 0.005.
Values may be sent and summed in bfloat16 or wider, within the bound.
A program may use at most 64 MiB of HBM per device.

```python
import math
import jax
import jax.numpy as jnp
import numpy as np
from jax import lax

D = 3072
TEN = 8
RANK = 16
TOP = 2
CAP = 32
FF = 1024
EXPERTS = 4
TOKG = 48
TOKENS = 192
N_EXPERT = 4


def with_ends(result, stream_key, smallest, largest):
    index_at = [jax.random.randint(jax.random.fold_in(stream_key, axis), (), 0, length) for axis, length in enumerate(result.shape)]
    main_axis = result.shape.index(max(result.shape))
    neighbour = index_at[:main_axis] + [(index_at[main_axis] + 1) % result.shape[main_axis]] + index_at[main_axis + 1:]
    return result.at[tuple(index_at)].set(smallest).at[tuple(neighbour)].set(largest)


def block_scale(key, dims, split, smallest, largest):
    gain = 1.0
    for dim, parts in split:
        heights = jax.random.uniform(jax.random.fold_in(jax.random.fold_in(key, 6), dim), (parts,), jnp.float32, smallest / len(split), largest / len(split))
        gain = gain * jnp.repeat(jnp.exp(heights), dims[dim] // parts).reshape((-1,) + (1,) * (len(dims) - 1 - dim))
    return gain


def assign_block(rng, own, number, rows, amount, top, most, skew):
    ranking = jax.random.permutation(rng, amount)
    packed, ordinary = shares(amount, rows * top, most, skew, True), shares(amount, rows * top, most, skew, False)
    places = jnp.arange(amount)

    def named(sizes, offset_by):
        used = int((sizes > 0).sum())
        fixed = max(1, used // 4)
        moved = fixed + (places - fixed + offset_by * (used - fixed)) % max(1, amount - fixed)
        return jnp.zeros((amount,), jnp.int32).at[ranking[jnp.where(places < fixed, places, moved)]].set(jnp.asarray(sizes, jnp.int32))

    sizes = jnp.where(number % 4 == 0, named(packed, number // 4), named(ordinary, number - number // 4 - 1))
    mixed = jax.random.permutation(jax.random.fold_in(own, 3), amount)
    donor, taker = mixed[0:amount // 2 * 2:2], mixed[1:amount // 2 * 2:2]
    margin = jnp.minimum(sizes[donor] - 1, most - sizes[taker]) // 2
    margin = jnp.where((donor == ranking[0]) | (taker == ranking[0]) | (sizes[taker] == 0), 0, jnp.maximum(margin, 0))
    moved = jax.random.randint(jax.random.fold_in(own, 4), (amount // 2,), 0, 1 << 20) % (margin + 1)
    sizes = sizes.at[donor].add(-moved).at[taker].add(moved)
    members = jnp.searchsorted(jnp.cumsum(sizes), jnp.arange(rows * top), side="right").astype(jnp.int32)
    listing = members.reshape(top, rows).T
    listing = listing[jax.random.permutation(jax.random.fold_in(own, 1), rows)]
    offset_by = jax.random.randint(jax.random.fold_in(own, 2), (rows, 1), 0, top)
    return jnp.take_along_axis(listing, (jnp.arange(top)[None, :] + offset_by) % top, axis=1)


def shares(amount, total, most, skew, full):
    weights = [(1 << 20) // math.isqrt(grade ** skew) + 1 for grade in range(1, amount + 1)]
    largest = most if full else min(most, max(-(-total // amount), total * weights[0] // sum(weights)))
    least = 1 if total - largest >= amount - 1 else 0
    given, surplus = [largest] + [least] * (amount - 1), total - largest - least * (amount - 1)
    while surplus > 0:
        candidates = [i for i in range(1, amount) if given[i] < largest] or [i for i in range(1, amount) if given[i] < most]
        pool, remaining = sum([weights[i] for i in candidates]), surplus
        for i in candidates:
            addition = min(most - given[i], max(1, remaining * weights[i] // pool), surplus)
            given[i] = given[i] + addition
            surplus = surplus - addition
    return np.array(given)


def scatter_about(own_key, shape, width, most, pieces=(), kind=jnp.bfloat16):
    result = jax.random.normal(own_key, shape, jnp.float32) * width
    if len(pieces) > 0:
        result = block_scale(own_key, shape, pieces, -0.22, 0.18) * result
    return jnp.clip(result, min=-most, max=most).astype(kind)


def setup_inputs(seed: int = 0) -> dict:
    splits = jax.random.split(jax.random.key(seed), 11)
    tokens = scatter_about(splits[0], (TOKENS, D), 1.0, 6.0, ((0, 4), (1, 2)))
    cotangent = scatter_about(splits[1], (TOKENS, D), 1.0, 6.0, ((0, 4), (1, 2)))
    expert_ids_keys = jax.random.split(jax.random.fold_in(splits[2], 1), TOKENS // TOKG)
    expert_ids_turns = jax.random.permutation(jax.random.fold_in(splits[2], 3), TOKENS // TOKG)
    expert_ids = jax.vmap(lambda own, number: assign_block(jax.random.fold_in(splits[2], 2), own, number, TOKG, EXPERTS, TOP, CAP, 2))(expert_ids_keys, expert_ids_turns).reshape((TOKENS, TOP))
    gate_probs = jnp.clip(0.049804688 + 0.89941406 * jax.random.uniform(splits[3], (TOKENS, TOP), jnp.float32) ** block_scale(splits[3], (TOKENS, TOP), ((0, 4),), -0.2, 0.2), 0.049804688, 0.94921875).astype(jnp.bfloat16)
    tenant_ids = with_ends(jax.random.randint(splits[4], (TOKENS,), 0, TEN), jax.random.fold_in(splits[4], 1), 0, TEN - 1).astype(jnp.int32)
    w_gate = scatter_about(splits[5], (EXPERTS, D, FF), D ** -0.5, 0.109375, ((0, 4), (2, 8)))
    w_up = scatter_about(splits[6], (EXPERTS, D, FF), D ** -0.5, 0.109375, ((0, 4), (2, 8)))
    w_down = scatter_about(splits[7], (EXPERTS, FF, D), FF ** -0.5, 0.1875, ((0, 4), (1, 8)))
    adapter_in = scatter_about(splits[8], (EXPERTS, FF, TEN * RANK), FF ** -0.5, 0.1875, ((0, 4), (1, 8)))
    adapter_out = scatter_about(splits[9], (EXPERTS, TEN * RANK, D), D ** -0.5, 0.109375, ((0, 4),))
    return {"tokens": tokens, "cotangent": cotangent, "expert_ids": expert_ids, "gate_probs": gate_probs, "tenant_ids": tenant_ids, "w_gate": w_gate, "w_up": w_up, "w_down": w_down, "adapter_in": adapter_in, "adapter_out": adapter_out}


adapter_scale_factor = 2.0


def reference(tokens, cotangent, expert_ids, gate_probs, tenant_ids, w_gate, w_up, w_down, adapter_in, adapter_out):
    groups = N_EXPERT
    slot_count = N_EXPERT * CAP
    route_ids = expert_ids.reshape(groups, TOKG * TOP)
    onehot = (route_ids[:, :, None] == jnp.arange(EXPERTS, dtype=jnp.int32)[None, None, :]).astype(jnp.int32)
    earlier = jnp.cumsum(onehot, axis=1) - onehot
    slot_index = jnp.sum(earlier * onehot, axis=2)
    group_index = jnp.arange(groups, dtype=jnp.int32)[:, None]
    row_index = (group_index * CAP + slot_index).astype(jnp.int32)
    token_index = (group_index * TOKG + jnp.arange(TOKG * TOP, dtype=jnp.int32)[None, :] // TOP).astype(jnp.int32)
    inputs = jnp.zeros((EXPERTS, slot_count, D), jnp.bfloat16).at[route_ids, row_index].set(tokens[token_index])
    grads = jnp.zeros((EXPERTS, slot_count, D), jnp.bfloat16).at[route_ids, row_index].set(cotangent[token_index])
    weights = jnp.zeros((EXPERTS, slot_count), jnp.float32).at[route_ids, row_index].set(
        gate_probs.reshape(groups, TOKG * TOP).astype(jnp.float32))
    tenants = jnp.zeros((EXPERTS, slot_count), jnp.int32).at[route_ids, row_index].set(tenant_ids[token_index])
    column_tenant = jnp.arange(TEN * RANK, dtype=jnp.int32) // RANK

    def per_expert(items):
        x_rows, y_rows, weight_rows_matrix, t_rows, wg, wu, wd, a_in, a_out = items
        gate_val = jnp.dot(x_rows, wg, preferred_element_type=jnp.float32)
        up_val = jnp.dot(x_rows, wu, preferred_element_type=jnp.float32)
        sig = jax.nn.sigmoid(gate_val)
        silu_val = gate_val * sig
        hidden = (silu_val * up_val).astype(jnp.bfloat16)
        low_in = jnp.dot(hidden, a_in, preferred_element_type=jnp.float32)
        low_back = lax.dot_general(y_rows, a_out, (((1,), (1,)), ((), ())), preferred_element_type=jnp.float32)
        routing_flags = (t_rows[:, None] == column_tenant[None, :]).astype(jnp.float32)
        gate_weighted_rows = adapter_scale_factor * weight_rows_matrix[:, None] * routing_flags
        down_coef = (gate_weighted_rows * low_back).astype(jnp.bfloat16)
        up_coef = (gate_weighted_rows * low_in).astype(jnp.bfloat16)
        back = lax.dot_general(y_rows, wd, (((1,), (1,)), ((), ())), preferred_element_type=jnp.float32)
        hidden_gradient = weight_rows_matrix[:, None] * back + lax.dot_general(
            down_coef, a_in, (((1,), (1,)), ((), ())), preferred_element_type=jnp.float32)
        slope = sig * (1.0 + gate_val * (1.0 - sig))
        gate_grad = (hidden_gradient * up_val * slope).astype(jnp.bfloat16)
        up_grad = (hidden_gradient * silu_val).astype(jnp.bfloat16)
        row_grad = lax.dot_general(gate_grad, wg, (((1,), (1,)), ((), ())), preferred_element_type=jnp.float32)
        row_grad = row_grad + lax.dot_general(up_grad, wu, (((1,), (1,)), ((), ())), preferred_element_type=jnp.float32)
        grad_a = lax.dot_general(hidden, down_coef, (((0,), (0,)), ((), ())), preferred_element_type=jnp.float32)
        grad_b = lax.dot_general(up_coef, y_rows, (((0,), (0,)), ((), ())), preferred_element_type=jnp.float32)
        return row_grad, grad_a, grad_b

    row_grads, grad_in, grad_out = lax.map(
        per_expert, (inputs, grads, weights, tenants, w_gate, w_up, w_down, adapter_in, adapter_out))
    routed = row_grads[route_ids, row_index].reshape(groups, TOKG, TOP, D)
    total = routed[:, :, 0, :]
    for second in range(1, TOP):
        total = total + routed[:, :, second, :]
    input_grad = total.reshape(TOKENS, D).astype(jnp.bfloat16)
    return input_grad, grad_in, grad_out
```

```python
import functools

import jax
import jax.numpy as jnp
from jax import lax
from jax.experimental import pallas as pl
from jax.experimental.pallas import tpu as pltpu
from jax.sharding import PartitionSpec as P

TEN = 8
RANK = 16
TOP = 2
CAP = 32


adapter_scale_factor = 2.0


def on_device(
    tokens,
    cotangent,
    expert_ids,
    gate_probs,
    tenant_ids,
    w_gate,
    w_up,
    w_down,
    adapter_in,
    adapter_out,
):
    experts = lax.axis_size("expert")
    tok_rows = tokens.shape[0]
    col_width = tokens.shape[1]
    slot_count = experts * CAP
    route_ids = expert_ids.reshape(-1)
    route_total = route_ids.shape[0]
    onehot = (route_ids[:, None] == jnp.arange(experts, dtype=jnp.int32)[None, :]).astype(jnp.int32)
    earlier = jnp.cumsum(onehot, axis=0) - onehot
    slot_index = jnp.sum(earlier * onehot, axis=1)
    target = route_ids * CAP + slot_index
    owner_token = jnp.arange(route_total, dtype=jnp.int32) // TOP
    slot_hits = (target[None, :] == jnp.arange(slot_count, dtype=jnp.int32)[:, None]).astype(
        jnp.float32
    )
    token_hits = (owner_token[:, None] == jnp.arange(tok_rows, dtype=jnp.int32)[None, :]).astype(
        jnp.float32
    )
    dispatch = jnp.dot(slot_hits, token_hits, precision=lax.Precision.HIGHEST)
    tenant_hot = (tenant_ids[:, None] == jnp.arange(TEN, dtype=jnp.int32)[None, :]).astype(
        jnp.float32
    )
    route_weight = gate_probs.reshape(-1).astype(jnp.float32)
    route_marks = (
        jnp.dot(token_hits, tenant_hot, precision=lax.Precision.HIGHEST) * route_weight[:, None]
    )
    slot_marks = jnp.dot(slot_hits, route_marks, precision=lax.Precision.HIGHEST)
    dispatch_half = dispatch.astype(jnp.bfloat16)
    send_inputs = jnp.dot(dispatch_half, tokens, preferred_element_type=jnp.float32).astype(
        jnp.bfloat16
    )
    send_grads = jnp.dot(dispatch_half, cotangent, preferred_element_type=jnp.float32).astype(
        jnp.bfloat16
    )
    send_inputs = send_inputs.reshape(experts, CAP, col_width)
    send_grads = send_grads.reshape(experts, CAP, col_width)
    send_marks = slot_marks.astype(jnp.bfloat16).reshape(experts, CAP, TEN)
    recv_inputs, recv_grads, recv_marks = (
        lax.all_to_all(send_inputs, "expert", split_axis=0, concat_axis=0, tiled=True),
        lax.all_to_all(send_grads, "expert", split_axis=0, concat_axis=0, tiled=True),
        lax.all_to_all(send_marks, "expert", split_axis=0, concat_axis=0, tiled=True),
    )
    gate_mat = w_gate[0]
    up_mat = w_up[0]
    down_mat = w_down[0]
    first_factor = adapter_in[0]
    second_factor = adapter_out[0]
    hidden_units = gate_mat.shape[1]
    low_width = first_factor.shape[1]
    input_piece = lax.all_gather(recv_inputs, "tensor", axis=2, tiled=True)
    grad_piece = lax.all_gather(recv_grads, "tensor", axis=2, tiled=True)
    piece_width = input_piece.shape[2]
    input_piece = input_piece.reshape(slot_count, piece_width)
    grad_piece = grad_piece.reshape(slot_count, piece_width)
    gate_rows = gate_mat
    up_projection_rows = up_mat
    gate_acc = jnp.dot(input_piece, gate_rows, preferred_element_type=jnp.float32)
    up_acc = jnp.dot(input_piece, up_projection_rows, preferred_element_type=jnp.float32)
    back_acc = lax.dot_general(
        grad_piece, down_mat, (((1,), (1,)), ((), ())), preferred_element_type=jnp.float32
    )
    low_acc = lax.dot_general(
        grad_piece, second_factor, (((1,), (1,)), ((), ())), preferred_element_type=jnp.float32
    )
    sig = jax.nn.sigmoid(gate_acc)
    silu_val = gate_acc * sig
    hidden = (silu_val * up_acc).astype(jnp.bfloat16)
    low_part = jnp.dot(hidden, first_factor, preferred_element_type=jnp.float32)
    marks_value = recv_marks.reshape(slot_count, TEN).astype(jnp.float32)
    row_weight = jnp.sum(marks_value, axis=1)
    broadcast_routing_flags = jnp.repeat(marks_value, RANK, axis=1)
    low_in = lax.psum(low_part, ("dp", "tensor"))
    gate_weighted_rows = adapter_scale_factor * broadcast_routing_flags
    down_coef = (gate_weighted_rows * low_acc).astype(jnp.bfloat16)
    up_coef = (gate_weighted_rows * low_in).astype(jnp.bfloat16)
    hidden_gradient = row_weight[:, None] * back_acc + lax.dot_general(
        down_coef, first_factor, (((1,), (1,)), ((), ())), preferred_element_type=jnp.float32
    )
    slope = sig * (1.0 + gate_acc * (1.0 - sig))
    gate_grad = (hidden_gradient * up_acc * slope).astype(jnp.bfloat16)
    up_grad = (hidden_gradient * silu_val).astype(jnp.bfloat16)
    grad_a = lax.dot_general(
        hidden, down_coef, (((0,), (0,)), ((), ())), preferred_element_type=jnp.float32
    )
    local_grads = recv_grads.reshape(slot_count, col_width)
    grad_b = lax.dot_general(
        up_coef, local_grads, (((0,), (0,)), ((), ())), preferred_element_type=jnp.float32
    )
    gate_rows = gate_mat
    up_projection_rows = up_mat
    term = lax.dot_general(
        gate_rows, gate_grad, (((1,), (1,)), ((), ())), preferred_element_type=jnp.float32
    )
    slices = lax.psum_scatter(
        term
        + lax.dot_general(
            up_projection_rows,
            up_grad,
            (((1,), (1,)), ((), ())),
            preferred_element_type=jnp.float32,
        ),
        ("dp", "tensor"),
        scatter_dimension=0,
        tiled=True,
    )
    slice_width = slices.shape[0]
    returned = lax.all_to_all(
        slices.reshape(slice_width, experts, CAP), "expert", split_axis=1, concat_axis=1, tiled=True
    )
    returned = returned.reshape(slice_width, slot_count)
    token_grad = lax.dot_general(
        dispatch,
        returned,
        (((0,), (1,)), ((), ())),
        precision=lax.Precision.HIGHEST,
        preferred_element_type=jnp.float32,
    )
    input_grad = token_grad.astype(jnp.bfloat16)
    return (
        input_grad,
        grad_a.reshape(1, hidden_units, low_width),
        grad_b.reshape(1, low_width, col_width),
    )


MESH = pl.DeviceIdType.MESH
LANES = 128
F32 = jnp.float32
BF16 = jnp.bfloat16


def partner(index, step):
    bit = 1
    while bit <= step:
        if step & bit:
            index = index + bit - 2 * bit * lax.rem(lax.div(index, bit), 2)
        bit *= 2
    return index


def tdot(a, b):
    return lax.dot_general(a, b, (((0,), (0,)), ((), ())), preferred_element_type=F32)


def ndot(a, b):
    return lax.dot_general(a, b, (((1,), (1,)), ((), ())), preferred_element_type=F32)


def layer_kernel(
    sizes,
    tok_ref, cot_ref, ids_ref, prob_ref, ten_ref, wg_ref, wu_ref, wd_ref, ain_ref, aout_ref,
    dx_ref, ga_ref, gb_ref,
    rows, send, wgu, wgb, wda, ain, mine, theirs, hid, grads, out_part, in_part, back_send, back, kept, low_mine, low_theirs,
    local_sem, w_send, w_recv, z_send, z_recv, p_send, p_recv, s_send, s_recv,
    r_send, r_recv, b_send, b_recv, l_send, l_recv,
):
    dp, ex, tn = sizes
    d, e, t = lax.axis_index("dp"), lax.axis_index("expert"), lax.axis_index("tensor")
    tokg, half = tok_ref.shape
    wide = half // dp
    ff = wg_ref.shape[3]
    low = ain_ref.shape[2]
    hall = tn * ff
    slots = ex * CAP

    barrier = pltpu.get_barrier_semaphore()
    for axis, index, count in (("tensor", t, tn), ("dp", d, dp), ("expert", e, ex)):
        for step in range(1, count):
            pl.semaphore_signal(
                barrier, inc=1, device_id={axis: partner(index, step)}, device_id_type=MESH
            )

    def remote(src, dst, ssem, rsem, axis, to):
        return pltpu.make_async_remote_copy(
            src_ref=src, dst_ref=dst, send_sem=ssem, recv_sem=rsem,
            device_id={axis: to}, device_id_type=MESH,
        )

    def lanes(start, size):
        return pl.ds(pl.multiple_of(start, LANES), size)

    def weight_parts(feat_owner, hid_owner):
        f = lanes(feat_owner * half, half)
        run = pl.ds(feat_owner * (dp // tn), dp // tn)
        gate_cols, up_cols = lanes(hid_owner * ff, ff), lanes(hall + hid_owner * ff, ff)
        return (
            (wg_ref.at[run], wgu.at[:, :, :, gate_cols]),
            (wu_ref.at[run], wgu.at[:, :, :, up_cols]),
            (wd_ref.at[0, :, f], wda.at[lanes(hid_owner * ff, ff), :]),
            (ain_ref.at[0], ain.at[lanes(hid_owner * ff, ff), :]),
            (wg_ref.at[:, feat_owner], wgb.at[:, :, gate_cols]),
            (wu_ref.at[:, feat_owner], wgb.at[:, :, up_cols]),
        )

    local = [
        pltpu.make_async_copy(s, o, local_sem.at[i])
        for i, (s, o) in enumerate(weight_parts(t, t))
    ]
    local.append(
        pltpu.make_async_copy(aout_ref.at[0, :, lanes(t * half, half)], wda.at[pl.ds(hall, low), :], local_sem.at[len(local)])
    )
    for c in local:
        c.start()

    ti = lax.broadcasted_iota(jnp.int32, (tokg, tokg), 0)
    tj = lax.broadcasted_iota(jnp.int32, (tokg, tokg), 1)

    def column(row):
        wide_row = jnp.broadcast_to(row.astype(F32), (tokg, tokg))
        return jnp.sum(jnp.where(ti == tj, wide_row, 0.0), axis=1, keepdims=True)

    ids0, ids1 = column(ids_ref[0:1, :]).astype(jnp.int32), column(ids_ref[1:2, :]).astype(jnp.int32)
    probs = prob_ref[...].astype(F32)
    prob0, prob1 = column(probs[0:1, :]), column(probs[1:2, :])
    col = lax.broadcasted_iota(jnp.int32, (tokg, slots), 1)
    ecol = lax.div(col, CAP)
    scol = col - ecol * CAP
    hit0, hit1 = ids0 == ecol, ids1 == ecol
    named = jnp.where(hit0 | hit1, 1.0, 0.0)
    before = jnp.where(ti > tj, 1.0, 0.0).astype(BF16)
    place = jnp.dot(before, named.astype(BF16), preferred_element_type=F32)
    disp = jnp.where(place == scol.astype(F32), named, 0.0)
    weight = jnp.where(hit0, prob0, 0.0) + jnp.where(hit1, prob1, 0.0)
    tcol = column(ten_ref[...])
    lowcol = lax.div(lax.broadcasted_iota(jnp.int32, (tokg, low), 1), RANK).astype(F32)
    tmark = jnp.where(tcol == lowcol, 1.0, 0.0).astype(BF16)
    marks = tdot((disp * weight).astype(BF16), tmark).astype(BF16)
    disp = disp.astype(BF16)
    mycols = lanes(d * wide, wide)
    sx = tdot(disp, tok_ref[:, mycols]).astype(BF16)
    sy = tdot(disp, cot_ref[:, mycols]).astype(BF16)
    send[:, :, 0:wide] = sx.reshape(ex, CAP, wide)
    send[:, :, wide:2 * wide] = sy.reshape(ex, CAP, wide)
    send[:, :, 2 * wide:] = marks.reshape(ex, CAP, low)

    pl.semaphore_wait(barrier, (tn - 1) + (dp - 1) + (ex - 1))

    sends = []
    for step in range(1, ex):
        to = partner(e, step)
        c = remote(send.at[to], rows.at[e, d], z_send.at[step], z_recv.at[e], "expert", to)
        c.start()
        sends.append(c)
    for step in range(1, tn):
        to = partner(t, step)
        for i, (s, o) in enumerate(weight_parts(to, t)):
            c = remote(s, o, w_send.at[step, i], w_recv.at[t, i], "tensor", to)
            c.start()
            sends.append(c)

    scol_own = lax.broadcasted_iota(jnp.int32, (tokg, CAP), 1).astype(F32)
    named_own = jnp.where((ids0 == e) | (ids1 == e), 1.0, 0.0)
    named_own = jnp.broadcast_to(named_own, (tokg, CAP))
    place_own = jnp.dot(before, named_own.astype(BF16), preferred_element_type=F32)
    disp_own = jnp.where(place_own == scol_own, named_own, 0.0).astype(BF16)
    for k in range(dp):
        cols = slice(k * wide, (k + 1) * wide)
        rows[e, k, :, 0:wide] = tdot(disp_own, tok_ref[:, cols]).astype(BF16)
        rows[e, k, :, wide:2 * wide] = tdot(disp_own, cot_ref[:, cols]).astype(BF16)
    rows[e, d, :, 2 * wide:] = send[e, :, 2 * wide:]

    for step in range(1, ex):
        g = partner(e, step)
        remote(send.at[g], rows.at[g, d], z_send.at[step], z_recv.at[g], "expert", g).wait_recv()
        for hop in range(1, dp):
            to = partner(d, hop)
            part = rows.at[g, d, :, pl.ds(0, 2 * wide)]
            c = remote(part, part, p_send.at[step, hop], p_recv.at[g, d], "dp", to)
            c.start()
            sends.append(c)

    for c in local:
        c.wait()
    for step in range(1, tn):
        frm = partner(t, step)
        for i, (s, o) in enumerate(weight_parts(t, frm)):
            remote(s, o, w_send.at[step, i], w_recv.at[frm, i], "tensor", frm).wait_recv()

    def products(g):
        gu = jnp.zeros((CAP, 2 * hall), F32)
        bl = jnp.zeros((CAP, hall + low), F32)
        for k in range(dp):
            f = slice(k * wide, (k + 1) * wide)
            gu = gu + jnp.dot(rows[g, k, :, 0:wide], wgu[k // tn, k % tn], preferred_element_type=F32)
            bl = bl + ndot(rows[g, k, :, wide:2 * wide], wda[:, f])
        mine[g, :, 0:2 * hall] = gu
        mine[g, :, 2 * hall:] = bl
        for hop in range(1, tn):
            to = partner(t, hop)
            c = remote(mine.at[g], theirs.at[t, g], s_send.at[hop, step], s_recv.at[t, g], "tensor", to)
            c.start()
            sends.append(c)

    for step in range(ex):
        g = partner(e, step)
        if step:
            for hop in range(1, dp):
                frm = partner(d, hop)
                part = rows.at[g, frm, :, pl.ds(0, 2 * wide)]
                remote(part, part, p_send.at[step, hop], p_recv.at[g, frm], "dp", frm).wait_recv()
        products(g)

    for step in range(ex):
        g = partner(e, step)
        for hop in range(1, tn):
            frm = partner(t, hop)
            remote(mine.at[g], theirs.at[frm, g], s_send.at[hop, step], s_recv.at[frm, g], "tensor", frm).wait_recv()
    total = mine[...].reshape(slots, -1)
    for hop in range(1, tn):
        total = total + theirs[partner(t, hop)].reshape(slots, -1)
    gate, up = total[:, 0:hall], total[:, hall:2 * hall]
    back_acc, low_acc = total[:, 2 * hall:3 * hall], total[:, 3 * hall:]
    flags = rows[:, d, :, 2 * wide:].reshape(slots, low).astype(F32)
    row_weight = jnp.max(flags, axis=1, keepdims=True)
    flags = adapter_scale_factor * flags
    sig = jax.nn.sigmoid(gate)
    silu = gate * sig
    hidden = (silu * up).astype(BF16)
    hid[...] = hidden
    down_coef = (flags * low_acc).astype(BF16)
    a_in = ain[...]
    hidden_grad = row_weight * back_acc + ndot(down_coef, a_in)
    slope = sig * (1.0 + gate * (1.0 - sig))
    grads[:, 0:hall] = (hidden_grad * up * slope).astype(BF16)
    grads[:, hall:] = (hidden_grad * silu).astype(BF16)

    def slice_grad(k):
        return ndot(grads[...], wgb[k])

    for hop in range(dp - 1, 0, -1):
        to = partner(d, hop)
        out_part[hop] = slice_grad(to).astype(BF16).reshape(ex, CAP, wide)
        for step in range(ex - 1, -1, -1):
            g = partner(e, step)
            c = remote(out_part.at[hop, g], in_part.at[d, g], r_send.at[hop, step], r_recv.at[d, g], "dp", to)
            c.start()
            sends.append(c)
    own = slice_grad(d).reshape(ex, CAP, wide)
    low_mine[...] = jnp.dot(hidden, a_in, preferred_element_type=F32)
    for hop in range(1, dp):
        c = remote(low_mine, low_theirs.at[d], l_send.at[hop], l_recv.at[d], "dp", partner(d, hop))
        c.start()
        sends.append(c)
    kept[...] = own
    ga_ref[0] = tdot(hid[:, lanes(t * ff, ff)], down_coef)

    for step in range(ex - 1, -1, -1):
        g = partner(e, step)
        acc = kept[g]
        for hop in range(dp - 1, 0, -1):
            frm = partner(d, hop)
            remote(out_part.at[hop, g], in_part.at[frm, g], r_send.at[hop, step], r_recv.at[frm, g], "dp", frm).wait_recv()
            acc = acc + in_part[frm, g].astype(F32)
        if step:
            back_send[step] = acc.astype(BF16)
            c = remote(back_send.at[step], back.at[e], b_send.at[step], b_recv.at[e], "expert", g)
            c.start()
            sends.append(c)
        else:
            back[e] = acc.astype(BF16)

    low_in = low_mine[...]
    for hop in range(1, dp):
        frm = partner(d, hop)
        remote(low_mine, low_theirs.at[frm], l_send.at[hop], l_recv.at[frm], "dp", frm).wait_recv()
    low_in = low_in + sum(low_theirs[partner(d, hop)] for hop in range(1, dp))
    up_coef = (flags * low_in).astype(BF16)
    for k in range(dp):
        y = rows[:, k, :, wide:2 * wide].reshape(slots, wide)
        gb_ref[0, :, k * wide:(k + 1) * wide] = tdot(up_coef, y)

    for step in range(1, ex):
        g = partner(e, step)
        remote(back_send.at[step], back.at[g], b_send.at[step], b_recv.at[g], "expert", g).wait_recv()
    dx_ref[...] = jnp.dot(disp, back[...].reshape(slots, wide), preferred_element_type=F32).astype(BF16)
    for c in sends:
        c.wait_send()


def fused(sizes, tokens, cotangent, expert_ids, gate_probs, tenant_ids, w_gate, w_up, w_down, adapter_in, adapter_out):
    dp, ex, tn = sizes
    tokg, half = tokens.shape
    wide = half // dp
    ff = w_gate.shape[2]
    low = adapter_in.shape[2]
    hall, slots = tn * ff, ex * CAP
    vmem, hbm = pl.BlockSpec(memory_space=pltpu.VMEM), pl.BlockSpec(memory_space=pl.ANY)
    dma = pltpu.SemaphoreType.DMA
    return pl.pallas_call(
        functools.partial(layer_kernel, sizes),
        out_shape=(
            jax.ShapeDtypeStruct((tokg, wide), BF16),
            jax.ShapeDtypeStruct((1, ff, low), F32),
            jax.ShapeDtypeStruct((1, low, half), F32),
        ),
        in_specs=[vmem] * 5 + [hbm] * 5,
        out_specs=(vmem, vmem, vmem),
        scratch_shapes=[
            pltpu.VMEM((ex, dp, CAP, 2 * wide + low), BF16),
            pltpu.VMEM((ex, CAP, 2 * wide + low), BF16),
            pltpu.VMEM((dp // tn, tn, wide, 2 * hall), BF16),
            pltpu.VMEM((dp, wide, 2 * hall), BF16),
            pltpu.VMEM((hall + low, half), BF16),
            pltpu.VMEM((hall, low), BF16),
            pltpu.VMEM((ex, CAP, 3 * hall + low), F32),
            pltpu.VMEM((tn, ex, CAP, 3 * hall + low), F32),
            pltpu.VMEM((slots, hall), BF16),
            pltpu.VMEM((slots, 2 * hall), BF16),
            pltpu.VMEM((dp, ex, CAP, wide), BF16),
            pltpu.VMEM((dp, ex, CAP, wide), BF16),
            pltpu.VMEM((ex, CAP, wide), BF16),
            pltpu.VMEM((ex, CAP, wide), BF16),
            pltpu.VMEM((ex, CAP, wide), F32),
            pltpu.VMEM((slots, low), F32),
            pltpu.VMEM((dp, slots, low), F32),
            dma((7,)),
            dma((tn, 6)), dma((tn, 6)),
            dma((ex,)), dma((ex,)),
            dma((ex, dp)), dma((ex, dp)),
            dma((tn, ex)), dma((tn, ex)),
            dma((dp, ex)), dma((dp, ex)),
            dma((ex,)), dma((ex,)),
            dma((dp,)), dma((dp,)),
        ],
        compiler_params=pltpu.CompilerParams(
            collective_id=0, has_side_effects=True, vmem_limit_bytes=40 * 1024 * 1024
        ),
        cost_estimate=pl.CostEstimate(flops=10**9, bytes_accessed=8 * 10**6, transcendentals=10**5),
    )(tokens, cotangent, expert_ids.T, gate_probs.T, tenant_ids.reshape(1, -1), w_gate.reshape(dp, tn, wide, ff), w_up.reshape(dp, tn, wide, ff), w_down, adapter_in, adapter_out)


def body_for(mesh):
    sizes = (mesh.shape["dp"], mesh.shape["expert"], mesh.shape["tensor"])
    paired = all(n & (n - 1) == 0 for n in sizes)

    def body(tokens, *rest):
        if paired and sizes[0] % sizes[2] == 0 and tokens.shape[1] % (sizes[0] * LANES) == 0:
            return fused(sizes, tokens, *rest)
        return on_device(tokens, *rest)

    return body


def solution(mesh):
    placed = (
        P("expert", "tensor"),
        P("expert", "tensor"),
        P("expert", None),
        P("expert", None),
        P("expert"),
        P("expert", None, ("dp", "tensor")),
        P("expert", None, ("dp", "tensor")),
        P("expert", ("dp", "tensor"), None),
        P("expert", ("dp", "tensor"), None),
        P("expert", None, None),
    )
    return jax.shard_map(
        body_for(mesh),
        mesh=mesh,
        in_specs=placed,
        out_specs=(
            P("expert", ("dp", "tensor")),
            P("expert", ("dp", "tensor"), None),
            P("expert", None, "tensor"),
        ),
        check_vma=False,
    )
```

```python
import functools

import jax
import jax.numpy as jnp
from jax import lax
from jax.experimental import pallas as pl
from jax.experimental.pallas import tpu as pltpu
from jax.sharding import PartitionSpec as P

TEN = 8
RANK = 16
TOP = 2
CAP = 32


adapter_scale_factor = 2.0


def on_device(
    tokens,
    cotangent,
    expert_ids,
    gate_probs,
    tenant_ids,
    w_gate,
    w_up,
    w_down,
    adapter_in,
    adapter_out,
):
    experts = lax.axis_size("expert")
    tok_rows = tokens.shape[0]
    col_width = tokens.shape[1]
    slot_count = experts * CAP
    route_ids = expert_ids.reshape(-1)
    route_total = route_ids.shape[0]
    onehot = (route_ids[:, None] == jnp.arange(experts, dtype=jnp.int32)[None, :]).astype(jnp.int32)
    earlier = jnp.cumsum(onehot, axis=0) - onehot
    slot_index = jnp.sum(earlier * onehot, axis=1)
    target = route_ids * CAP + slot_index
    owner_token = jnp.arange(route_total, dtype=jnp.int32) // TOP
    slot_hits = (target[None, :] == jnp.arange(slot_count, dtype=jnp.int32)[:, None]).astype(
        jnp.float32
    )
    token_hits = (owner_token[:, None] == jnp.arange(tok_rows, dtype=jnp.int32)[None, :]).astype(
        jnp.float32
    )
    dispatch = jnp.dot(slot_hits, token_hits, precision=lax.Precision.HIGHEST)
    tenant_hot = (tenant_ids[:, None] == jnp.arange(TEN, dtype=jnp.int32)[None, :]).astype(
        jnp.float32
    )
    route_weight = gate_probs.reshape(-1).astype(jnp.float32)
    route_marks = (
        jnp.dot(token_hits, tenant_hot, precision=lax.Precision.HIGHEST) * route_weight[:, None]
    )
    slot_marks = jnp.dot(slot_hits, route_marks, precision=lax.Precision.HIGHEST)
    dispatch_half = dispatch.astype(jnp.bfloat16)
    send_inputs = jnp.dot(dispatch_half, tokens, preferred_element_type=jnp.float32).astype(
        jnp.bfloat16
    )
    send_grads = jnp.dot(dispatch_half, cotangent, preferred_element_type=jnp.float32).astype(
        jnp.bfloat16
    )
    send_inputs = send_inputs.reshape(experts, CAP, col_width)
    send_grads = send_grads.reshape(experts, CAP, col_width)
    send_marks = slot_marks.astype(jnp.bfloat16).reshape(experts, CAP, TEN)
    recv_inputs, recv_grads, recv_marks = (
        lax.all_to_all(send_inputs, "expert", split_axis=0, concat_axis=0, tiled=True),
        lax.all_to_all(send_grads, "expert", split_axis=0, concat_axis=0, tiled=True),
        lax.all_to_all(send_marks, "expert", split_axis=0, concat_axis=0, tiled=True),
    )
    gate_mat = w_gate[0]
    up_mat = w_up[0]
    down_mat = w_down[0]
    first_factor = adapter_in[0]
    second_factor = adapter_out[0]
    hidden_units = gate_mat.shape[1]
    low_width = first_factor.shape[1]
    input_piece = lax.all_gather(recv_inputs, "tensor", axis=2, tiled=True)
    grad_piece = lax.all_gather(recv_grads, "tensor", axis=2, tiled=True)
    piece_width = input_piece.shape[2]
    input_piece = input_piece.reshape(slot_count, piece_width)
    grad_piece = grad_piece.reshape(slot_count, piece_width)
    gate_rows = gate_mat
    up_projection_rows = up_mat
    gate_acc = jnp.dot(input_piece, gate_rows, preferred_element_type=jnp.float32)
    up_acc = jnp.dot(input_piece, up_projection_rows, preferred_element_type=jnp.float32)
    back_acc = lax.dot_general(
        grad_piece, down_mat, (((1,), (1,)), ((), ())), preferred_element_type=jnp.float32
    )
    low_acc = lax.dot_general(
        grad_piece, second_factor, (((1,), (1,)), ((), ())), preferred_element_type=jnp.float32
    )
    sig = jax.nn.sigmoid(gate_acc)
    silu_val = gate_acc * sig
    hidden = (silu_val * up_acc).astype(jnp.bfloat16)
    low_part = jnp.dot(hidden, first_factor, preferred_element_type=jnp.float32)
    marks_value = recv_marks.reshape(slot_count, TEN).astype(jnp.float32)
    row_weight = jnp.sum(marks_value, axis=1)
    broadcast_routing_flags = jnp.repeat(marks_value, RANK, axis=1)
    low_in = lax.psum(low_part, ("dp", "tensor"))
    gate_weighted_rows = adapter_scale_factor * broadcast_routing_flags
    down_coef = (gate_weighted_rows * low_acc).astype(jnp.bfloat16)
    up_coef = (gate_weighted_rows * low_in).astype(jnp.bfloat16)
    hidden_gradient = row_weight[:, None] * back_acc + lax.dot_general(
        down_coef, first_factor, (((1,), (1,)), ((), ())), preferred_element_type=jnp.float32
    )
    slope = sig * (1.0 + gate_acc * (1.0 - sig))
    gate_grad = (hidden_gradient * up_acc * slope).astype(jnp.bfloat16)
    up_grad = (hidden_gradient * silu_val).astype(jnp.bfloat16)
    grad_a = lax.dot_general(
        hidden, down_coef, (((0,), (0,)), ((), ())), preferred_element_type=jnp.float32
    )
    local_grads = recv_grads.reshape(slot_count, col_width)
    grad_b = lax.dot_general(
        up_coef, local_grads, (((0,), (0,)), ((), ())), preferred_element_type=jnp.float32
    )
    gate_rows = gate_mat
    up_projection_rows = up_mat
    term = lax.dot_general(
        gate_rows, gate_grad, (((1,), (1,)), ((), ())), preferred_element_type=jnp.float32
    )
    slices = lax.psum_scatter(
        term
        + lax.dot_general(
            up_projection_rows,
            up_grad,
            (((1,), (1,)), ((), ())),
            preferred_element_type=jnp.float32,
        ),
        ("dp", "tensor"),
        scatter_dimension=0,
        tiled=True,
    )
    slice_width = slices.shape[0]
    returned = lax.all_to_all(
        slices.reshape(slice_width, experts, CAP), "expert", split_axis=1, concat_axis=1, tiled=True
    )
    returned = returned.reshape(slice_width, slot_count)
    token_grad = lax.dot_general(
        dispatch,
        returned,
        (((0,), (1,)), ((), ())),
        precision=lax.Precision.HIGHEST,
        preferred_element_type=jnp.float32,
    )
    input_grad = token_grad.astype(jnp.bfloat16)
    return (
        input_grad,
        grad_a.reshape(1, hidden_units, low_width),
        grad_b.reshape(1, low_width, col_width),
    )


MESH = pl.DeviceIdType.MESH
LANES = 128
F32 = jnp.float32
BF16 = jnp.bfloat16


def partner(index, step):
    bit = 1
    while bit <= step:
        if step & bit:
            index = index + bit - 2 * bit * lax.rem(lax.div(index, bit), 2)
        bit *= 2
    return index


def tdot(a, b):
    return lax.dot_general(a, b, (((0,), (0,)), ((), ())), preferred_element_type=F32)


def ndot(a, b):
    return lax.dot_general(a, b, (((1,), (1,)), ((), ())), preferred_element_type=F32)


def layer_kernel(
    sizes,
    tok_hbm, cot_hbm, ids_hbm, prob_hbm, ten_hbm, wg_ref, wu_ref, wd_ref, ain_ref, aout_ref,
    dx_hbm, ga_hbm, gb_hbm,
    dx_ref, ga_ref, gb_ref, tok_ref, cot_ref, ids_ref, prob_ref, ten_ref, rows, send, wgu, wgb, wda, ain, mine, theirs, hid, grads, out_part, in_part, back_send, back, kept, low_mine, low_theirs,
    out_sem, in_sem, local_sem, w_send, w_recv, z_send, z_recv, p_send, p_recv, s_send, s_recv,
    r_send, r_recv, b_send, b_recv, l_send, l_recv,
):
    dp, ex, tn = sizes
    d, e, t = lax.axis_index("dp"), lax.axis_index("expert"), lax.axis_index("tensor")
    tokg, half = tok_hbm.shape
    wide = half // dp
    ff = wg_ref.shape[3]
    low = ain_ref.shape[2]
    hall = tn * ff
    slots = ex * CAP

    barrier = pltpu.get_barrier_semaphore()
    for axis, index, count in (("tensor", t, tn), ("dp", d, dp), ("expert", e, ex)):
        for step in range(1, count):
            pl.semaphore_signal(
                barrier, inc=1, device_id={axis: partner(index, step)}, device_id_type=MESH
            )

    loads = [
        pltpu.make_async_copy(s, o, in_sem.at[i])
        for i, (s, o) in enumerate(
            ((ids_hbm, ids_ref), (prob_hbm, prob_ref), (ten_hbm, ten_ref), (tok_hbm, tok_ref), (cot_hbm, cot_ref))
        )
    ]
    for c in loads:
        c.start()

    def remote(src, dst, ssem, rsem, axis, to):
        return pltpu.make_async_remote_copy(
            src_ref=src, dst_ref=dst, send_sem=ssem, recv_sem=rsem,
            device_id={axis: to}, device_id_type=MESH,
        )

    def lanes(start, size):
        return pl.ds(pl.multiple_of(start, LANES), size)

    def weight_parts(feat_owner, hid_owner):
        f = lanes(feat_owner * half, half)
        run = pl.ds(feat_owner * (dp // tn), dp // tn)
        gate_cols, up_cols = lanes(hid_owner * ff, ff), lanes(hall + hid_owner * ff, ff)
        return (
            (wg_ref.at[run], wgu.at[:, :, :, gate_cols]),
            (wu_ref.at[run], wgu.at[:, :, :, up_cols]),
            (wd_ref.at[0, :, f], wda.at[lanes(hid_owner * ff, ff), :]),
            (ain_ref.at[0], ain.at[lanes(hid_owner * ff, ff), :]),
            (wg_ref.at[:, feat_owner], wgb.at[:, :, gate_cols]),
            (wu_ref.at[:, feat_owner], wgb.at[:, :, up_cols]),
        )

    local = [
        pltpu.make_async_copy(s, o, local_sem.at[i])
        for i, (s, o) in enumerate(weight_parts(t, t))
    ]
    local.append(
        pltpu.make_async_copy(aout_ref.at[0, :, lanes(t * half, half)], wda.at[pl.ds(hall, low), :], local_sem.at[len(local)])
    )
    for c in local:
        c.start()

    for c in loads[:3]:
        c.wait()
    ti = lax.broadcasted_iota(jnp.int32, (tokg, tokg), 0)
    tj = lax.broadcasted_iota(jnp.int32, (tokg, tokg), 1)

    def column(row):
        wide_row = jnp.broadcast_to(row.astype(F32), (tokg, tokg))
        return jnp.sum(jnp.where(ti == tj, wide_row, 0.0), axis=1, keepdims=True)

    ids0, ids1 = column(ids_ref[0:1, :]).astype(jnp.int32), column(ids_ref[1:2, :]).astype(jnp.int32)
    probs = prob_ref[...].astype(F32)
    prob0, prob1 = column(probs[0:1, :]), column(probs[1:2, :])
    col = lax.broadcasted_iota(jnp.int32, (tokg, slots), 1)
    ecol = lax.div(col, CAP)
    scol = col - ecol * CAP
    hit0, hit1 = ids0 == ecol, ids1 == ecol
    named = jnp.where(hit0 | hit1, 1.0, 0.0)
    before = jnp.where(ti > tj, 1.0, 0.0).astype(BF16)
    place = jnp.dot(before, named.astype(BF16), preferred_element_type=F32)
    disp = jnp.where(place == scol.astype(F32), named, 0.0)
    weight = jnp.where(hit0, prob0, 0.0) + jnp.where(hit1, prob1, 0.0)
    tcol = column(ten_ref[...])
    lowcol = lax.div(lax.broadcasted_iota(jnp.int32, (tokg, low), 1), RANK).astype(F32)
    tmark = jnp.where(tcol == lowcol, 1.0, 0.0).astype(BF16)
    marks = tdot((disp * weight).astype(BF16), tmark).astype(BF16)
    disp = disp.astype(BF16)
    for c in loads[3:]:
        c.wait()
    mycols = lanes(d * wide, wide)
    sx = tdot(disp, tok_ref[:, mycols]).astype(BF16)
    sy = tdot(disp, cot_ref[:, mycols]).astype(BF16)
    send[:, :, 0:wide] = sx.reshape(ex, CAP, wide)
    send[:, :, wide:2 * wide] = sy.reshape(ex, CAP, wide)
    send[:, :, 2 * wide:] = marks.reshape(ex, CAP, low)

    pl.semaphore_wait(barrier, (tn - 1) + (dp - 1) + (ex - 1))

    sends = []
    z_parts = (pl.ds(0, wide), pl.ds(wide, wide + low))
    p_parts = (pl.ds(0, wide), pl.ds(wide, wide))
    for i, part in enumerate(z_parts):
        for step in range(1, ex):
            to = partner(e, step)
            c = remote(
                send.at[to, :, part], rows.at[e, d, :, part], z_send.at[step, i], z_recv.at[e, i], "expert", to
            )
            c.start()
            sends.append(c)
    for step in range(1, tn):
        to = partner(t, step)
        for i, (s, o) in enumerate(weight_parts(to, t)):
            c = remote(s, o, w_send.at[step, i], w_recv.at[t, i], "tensor", to)
            c.start()
            sends.append(c)

    scol_own = lax.broadcasted_iota(jnp.int32, (tokg, CAP), 1).astype(F32)
    named_own = jnp.where((ids0 == e) | (ids1 == e), 1.0, 0.0)
    named_own = jnp.broadcast_to(named_own, (tokg, CAP))
    place_own = jnp.dot(before, named_own.astype(BF16), preferred_element_type=F32)
    disp_own = jnp.where(place_own == scol_own, named_own, 0.0).astype(BF16)
    for k in range(dp):
        cols = slice(k * wide, (k + 1) * wide)
        rows[e, k, :, 0:wide] = tdot(disp_own, tok_ref[:, cols]).astype(BF16)
        rows[e, k, :, wide:2 * wide] = tdot(disp_own, cot_ref[:, cols]).astype(BF16)
    rows[e, d, :, 2 * wide:] = send[e, :, 2 * wide:]

    for i in range(2):
        for step in range(1, ex):
            g = partner(e, step)
            part = rows.at[g, d, :, z_parts[i]]
            remote(part, part, z_send.at[step, i], z_recv.at[g, i], "expert", g).wait_recv()
            for hop in range(1, dp):
                to = partner(d, hop)
                part = rows.at[g, d, :, p_parts[i]]
                c = remote(part, part, p_send.at[step, hop, i], p_recv.at[g, d, i], "dp", to)
                c.start()
                sends.append(c)

    for c in local:
        c.wait()
    for step in range(1, tn):
        frm = partner(t, step)
        for i, (s, o) in enumerate(weight_parts(t, frm)):
            remote(s, o, w_send.at[step, i], w_recv.at[frm, i], "tensor", frm).wait_recv()

    def products(g):
        gu = jnp.zeros((CAP, 2 * hall), F32)
        bl = jnp.zeros((CAP, hall + low), F32)
        for k in range(dp):
            f = slice(k * wide, (k + 1) * wide)
            gu = gu + jnp.dot(rows[g, k, :, 0:wide], wgu[k // tn, k % tn], preferred_element_type=F32)
            bl = bl + ndot(rows[g, k, :, wide:2 * wide], wda[:, f])
        mine[g, :, 0:2 * hall] = gu
        mine[g, :, 2 * hall:] = bl
        for hop in range(1, tn):
            to = partner(t, hop)
            c = remote(mine.at[g], theirs.at[t, g], s_send.at[hop, step], s_recv.at[t, g], "tensor", to)
            c.start()
            sends.append(c)

    for step in range(ex):
        g = partner(e, step)
        if step:
            for hop in range(1, dp):
                frm = partner(d, hop)
                for i in range(2):
                    part = rows.at[g, frm, :, p_parts[i]]
                    remote(part, part, p_send.at[step, hop, i], p_recv.at[g, frm, i], "dp", frm).wait_recv()
        products(g)

    for step in range(ex):
        g = partner(e, step)
        for hop in range(1, tn):
            frm = partner(t, hop)
            remote(mine.at[g], theirs.at[frm, g], s_send.at[hop, step], s_recv.at[frm, g], "tensor", frm).wait_recv()
    total = mine[...].reshape(slots, -1)
    for hop in range(1, tn):
        total = total + theirs[partner(t, hop)].reshape(slots, -1)
    gate, up = total[:, 0:hall], total[:, hall:2 * hall]
    back_acc, low_acc = total[:, 2 * hall:3 * hall], total[:, 3 * hall:]
    flags = rows[:, d, :, 2 * wide:].reshape(slots, low).astype(F32)
    row_weight = jnp.max(flags, axis=1, keepdims=True)
    flags = adapter_scale_factor * flags
    sig = jax.nn.sigmoid(gate)
    silu = gate * sig
    hidden = (silu * up).astype(BF16)
    hid[...] = hidden
    down_coef = (flags * low_acc).astype(BF16)
    a_in = ain[...]
    hidden_grad = row_weight * back_acc + ndot(down_coef, a_in)
    slope = sig * (1.0 + gate * (1.0 - sig))
    grads[:, 0:hall] = (hidden_grad * up * slope).astype(BF16)
    grads[:, hall:] = (hidden_grad * silu).astype(BF16)

    def slice_grad(k):
        return ndot(grads[...], wgb[k])

    for hop in range(dp - 1, 0, -1):
        to = partner(d, hop)
        out_part[hop] = slice_grad(to).astype(BF16).reshape(ex, CAP, wide)
        for step in range(ex - 1, -1, -1):
            g = partner(e, step)
            c = remote(out_part.at[hop, g], in_part.at[d, g], r_send.at[hop, step], r_recv.at[d, g], "dp", to)
            c.start()
            sends.append(c)
    own = slice_grad(d).reshape(ex, CAP, wide)
    low_part = jnp.dot(hidden, a_in, preferred_element_type=F32)
    low_mine[...] = low_part.astype(BF16)
    for hop in range(1, dp):
        c = remote(low_mine, low_theirs.at[d], l_send.at[hop], l_recv.at[d], "dp", partner(d, hop))
        c.start()
        sends.append(c)
    kept[...] = own
    ga_ref[...] = tdot(hid[:, lanes(t * ff, ff)], down_coef)
    results = [
        pltpu.make_async_copy(s, o, out_sem.at[i])
        for i, (s, o) in enumerate(((dx_ref, dx_hbm), (ga_ref, ga_hbm.at[0]), (gb_ref, gb_hbm.at[0])))
    ]
    results[1].start()

    for step in range(ex - 1, -1, -1):
        g = partner(e, step)
        acc = kept[g]
        for hop in range(dp - 1, 0, -1):
            frm = partner(d, hop)
            remote(out_part.at[hop, g], in_part.at[frm, g], r_send.at[hop, step], r_recv.at[frm, g], "dp", frm).wait_recv()
            acc = acc + in_part[frm, g].astype(F32)
        if step:
            back_send[step] = acc.astype(BF16)
            c = remote(back_send.at[step], back.at[e], b_send.at[step], b_recv.at[e], "expert", g)
            c.start()
            sends.append(c)
        else:
            back[e] = acc.astype(BF16)

    low_in = low_part
    for hop in range(1, dp):
        frm = partner(d, hop)
        remote(low_mine, low_theirs.at[frm], l_send.at[hop], l_recv.at[frm], "dp", frm).wait_recv()
    low_in = low_in + sum(low_theirs[partner(d, hop)].astype(F32) for hop in range(1, dp))
    up_coef = (flags * low_in).astype(BF16)
    for k in range(dp):
        y = rows[:, k, :, wide:2 * wide].reshape(slots, wide)
        gb_ref[:, k * wide:(k + 1) * wide] = tdot(up_coef, y)
    results[2].start()

    for step in range(1, ex):
        g = partner(e, step)
        remote(back_send.at[step], back.at[g], b_send.at[step], b_recv.at[g], "expert", g).wait_recv()
    dx_ref[...] = jnp.dot(disp, back[...].reshape(slots, wide), preferred_element_type=F32).astype(BF16)
    results[0].start()
    for c in sends:
        c.wait_send()
    for c in results:
        c.wait()


def write_kernel(a_ref, b_ref, c_ref, a_out, b_out, c_out, sem):
    copies = [
        pltpu.make_async_copy(s, o, sem.at[i])
        for i, (s, o) in enumerate(((c_ref, c_out), (b_ref, b_out), (a_ref, a_out)))
    ]
    for c in copies:
        c.start()
    for c in copies:
        c.wait()


def fused(sizes, tokens, cotangent, expert_ids, gate_probs, tenant_ids, w_gate, w_up, w_down, adapter_in, adapter_out):
    dp, ex, tn = sizes
    tokg, half = tokens.shape
    wide = half // dp
    ff = w_gate.shape[2]
    low = adapter_in.shape[2]
    hall, slots = tn * ff, ex * CAP
    hbm = pl.BlockSpec(memory_space=pltpu.HBM)
    dma = pltpu.SemaphoreType.DMA
    shapes = (
        jax.ShapeDtypeStruct((tokg, wide), BF16),
        jax.ShapeDtypeStruct((1, ff, low), F32),
        jax.ShapeDtypeStruct((1, low, half), F32),
    )
    results = pl.pallas_call(
        functools.partial(layer_kernel, sizes),
        out_shape=shapes,
        in_specs=[hbm] * 10,
        out_specs=(hbm, hbm, hbm),
        scratch_shapes=[
            pltpu.VMEM((tokg, wide), BF16),
            pltpu.VMEM((ff, low), F32),
            pltpu.VMEM((low, half), F32),
            pltpu.VMEM((tokg, half), BF16),
            pltpu.VMEM((tokg, half), BF16),
            pltpu.VMEM((TOP, tokg), jnp.int32),
            pltpu.VMEM((TOP, tokg), BF16),
            pltpu.VMEM((1, tokg), jnp.int32),
            pltpu.VMEM((ex, dp, CAP, 2 * wide + low), BF16),
            pltpu.VMEM((ex, CAP, 2 * wide + low), BF16),
            pltpu.VMEM((dp // tn, tn, wide, 2 * hall), BF16),
            pltpu.VMEM((dp, wide, 2 * hall), BF16),
            pltpu.VMEM((hall + low, half), BF16),
            pltpu.VMEM((hall, low), BF16),
            pltpu.VMEM((ex, CAP, 3 * hall + low), F32),
            pltpu.VMEM((tn, ex, CAP, 3 * hall + low), F32),
            pltpu.VMEM((slots, hall), BF16),
            pltpu.VMEM((slots, 2 * hall), BF16),
            pltpu.VMEM((dp, ex, CAP, wide), BF16),
            pltpu.VMEM((dp, ex, CAP, wide), BF16),
            pltpu.VMEM((ex, CAP, wide), BF16),
            pltpu.VMEM((ex, CAP, wide), BF16),
            pltpu.VMEM((ex, CAP, wide), F32),
            pltpu.VMEM((slots, low), BF16),
            pltpu.VMEM((dp, slots, low), BF16),
            dma((3,)), dma((5,)),
            dma((7,)),
            dma((tn, 6)), dma((tn, 6)),
            dma((ex, 2)), dma((ex, 2)),
            dma((ex, dp, 2)), dma((ex, dp, 2)),
            dma((tn, ex)), dma((tn, ex)),
            dma((dp, ex)), dma((dp, ex)),
            dma((ex,)), dma((ex,)),
            dma((dp,)), dma((dp,)),
        ],
        compiler_params=pltpu.CompilerParams(
            collective_id=0, has_side_effects=True, vmem_limit_bytes=62 * 1024 * 1024
        ),
        cost_estimate=pl.CostEstimate(flops=10**9, bytes_accessed=8 * 10**6, transcendentals=10**5),
    )(tokens, cotangent, expert_ids.T, gate_probs.T, tenant_ids.reshape(1, -1), w_gate.reshape(dp, tn, wide, ff), w_up.reshape(dp, tn, wide, ff), w_down, adapter_in, adapter_out)
    return pl.pallas_call(
        write_kernel,
        out_shape=shapes,
        in_specs=[hbm] * 3,
        out_specs=(hbm,) * 3,
        scratch_shapes=[dma((3,))],
        compiler_params=pltpu.CompilerParams(vmem_limit_bytes=62 * 1024 * 1024),
    )(*results)


def body_for(mesh):
    sizes = (mesh.shape["dp"], mesh.shape["expert"], mesh.shape["tensor"])
    paired = all(n & (n - 1) == 0 for n in sizes)

    def body(tokens, *rest):
        if paired and sizes[0] % sizes[2] == 0 and tokens.shape[1] % (sizes[0] * LANES) == 0:
            return fused(sizes, tokens, *rest)
        return on_device(tokens, *rest)

    return body


def solution(mesh):
    placed = (
        P("expert", "tensor"),
        P("expert", "tensor"),
        P("expert", None),
        P("expert", None),
        P("expert"),
        P("expert", None, ("dp", "tensor")),
        P("expert", None, ("dp", "tensor")),
        P("expert", ("dp", "tensor"), None),
        P("expert", ("dp", "tensor"), None),
        P("expert", None, None),
    )
    return jax.shard_map(
        body_for(mesh),
        mesh=mesh,
        in_specs=placed,
        out_specs=(
            P("expert", ("dp", "tensor")),
            P("expert", ("dp", "tensor"), None),
            P("expert", None, "tensor"),
        ),
        check_vma=False,
    )
```

```python
import functools

import jax
import jax.numpy as jnp
from jax import lax
from jax.experimental import pallas as pl
from jax.experimental.pallas import tpu as pltpu
from jax.sharding import PartitionSpec as P

TEN = 8
RANK = 16
TOP = 2
CAP = 32


adapter_scale_factor = 2.0


def on_device(
    tokens,
    cotangent,
    expert_ids,
    gate_probs,
    tenant_ids,
    w_gate,
    w_up,
    w_down,
    adapter_in,
    adapter_out,
):
    experts = lax.axis_size("expert")
    tok_rows = tokens.shape[0]
    col_width = tokens.shape[1]
    slot_count = experts * CAP
    route_ids = expert_ids.reshape(-1)
    route_total = route_ids.shape[0]
    onehot = (route_ids[:, None] == jnp.arange(experts, dtype=jnp.int32)[None, :]).astype(jnp.int32)
    earlier = jnp.cumsum(onehot, axis=0) - onehot
    slot_index = jnp.sum(earlier * onehot, axis=1)
    target = route_ids * CAP + slot_index
    owner_token = jnp.arange(route_total, dtype=jnp.int32) // TOP
    slot_hits = (target[None, :] == jnp.arange(slot_count, dtype=jnp.int32)[:, None]).astype(
        jnp.float32
    )
    token_hits = (owner_token[:, None] == jnp.arange(tok_rows, dtype=jnp.int32)[None, :]).astype(
        jnp.float32
    )
    dispatch = jnp.dot(slot_hits, token_hits, precision=lax.Precision.HIGHEST)
    tenant_hot = (tenant_ids[:, None] == jnp.arange(TEN, dtype=jnp.int32)[None, :]).astype(
        jnp.float32
    )
    route_weight = gate_probs.reshape(-1).astype(jnp.float32)
    route_marks = (
        jnp.dot(token_hits, tenant_hot, precision=lax.Precision.HIGHEST) * route_weight[:, None]
    )
    slot_marks = jnp.dot(slot_hits, route_marks, precision=lax.Precision.HIGHEST)
    dispatch_half = dispatch.astype(jnp.bfloat16)
    send_inputs = jnp.dot(dispatch_half, tokens, preferred_element_type=jnp.float32).astype(
        jnp.bfloat16
    )
    send_grads = jnp.dot(dispatch_half, cotangent, preferred_element_type=jnp.float32).astype(
        jnp.bfloat16
    )
    send_inputs = send_inputs.reshape(experts, CAP, col_width)
    send_grads = send_grads.reshape(experts, CAP, col_width)
    send_marks = slot_marks.astype(jnp.bfloat16).reshape(experts, CAP, TEN)
    recv_inputs, recv_grads, recv_marks = (
        lax.all_to_all(send_inputs, "expert", split_axis=0, concat_axis=0, tiled=True),
        lax.all_to_all(send_grads, "expert", split_axis=0, concat_axis=0, tiled=True),
        lax.all_to_all(send_marks, "expert", split_axis=0, concat_axis=0, tiled=True),
    )
    gate_mat = w_gate[0]
    up_mat = w_up[0]
    down_mat = w_down[0]
    first_factor = adapter_in[0]
    second_factor = adapter_out[0]
    hidden_units = gate_mat.shape[1]
    low_width = first_factor.shape[1]
    input_piece = lax.all_gather(recv_inputs, "tensor", axis=2, tiled=True)
    grad_piece = lax.all_gather(recv_grads, "tensor", axis=2, tiled=True)
    piece_width = input_piece.shape[2]
    input_piece = input_piece.reshape(slot_count, piece_width)
    grad_piece = grad_piece.reshape(slot_count, piece_width)
    gate_rows = gate_mat
    up_projection_rows = up_mat
    gate_acc = jnp.dot(input_piece, gate_rows, preferred_element_type=jnp.float32)
    up_acc = jnp.dot(input_piece, up_projection_rows, preferred_element_type=jnp.float32)
    back_acc = lax.dot_general(
        grad_piece, down_mat, (((1,), (1,)), ((), ())), preferred_element_type=jnp.float32
    )
    low_acc = lax.dot_general(
        grad_piece, second_factor, (((1,), (1,)), ((), ())), preferred_element_type=jnp.float32
    )
    sig = jax.nn.sigmoid(gate_acc)
    silu_val = gate_acc * sig
    hidden = (silu_val * up_acc).astype(jnp.bfloat16)
    low_part = jnp.dot(hidden, first_factor, preferred_element_type=jnp.float32)
    marks_value = recv_marks.reshape(slot_count, TEN).astype(jnp.float32)
    row_weight = jnp.sum(marks_value, axis=1)
    broadcast_routing_flags = jnp.repeat(marks_value, RANK, axis=1)
    low_in = lax.psum(low_part, ("dp", "tensor"))
    gate_weighted_rows = adapter_scale_factor * broadcast_routing_flags
    down_coef = (gate_weighted_rows * low_acc).astype(jnp.bfloat16)
    up_coef = (gate_weighted_rows * low_in).astype(jnp.bfloat16)
    hidden_gradient = row_weight[:, None] * back_acc + lax.dot_general(
        down_coef, first_factor, (((1,), (1,)), ((), ())), preferred_element_type=jnp.float32
    )
    slope = sig * (1.0 + gate_acc * (1.0 - sig))
    gate_grad = (hidden_gradient * up_acc * slope).astype(jnp.bfloat16)
    up_grad = (hidden_gradient * silu_val).astype(jnp.bfloat16)
    grad_a = lax.dot_general(
        hidden, down_coef, (((0,), (0,)), ((), ())), preferred_element_type=jnp.float32
    )
    local_grads = recv_grads.reshape(slot_count, col_width)
    grad_b = lax.dot_general(
        up_coef, local_grads, (((0,), (0,)), ((), ())), preferred_element_type=jnp.float32
    )
    gate_rows = gate_mat
    up_projection_rows = up_mat
    term = lax.dot_general(
        gate_rows, gate_grad, (((1,), (1,)), ((), ())), preferred_element_type=jnp.float32
    )
    slices = lax.psum_scatter(
        term
        + lax.dot_general(
            up_projection_rows,
            up_grad,
            (((1,), (1,)), ((), ())),
            preferred_element_type=jnp.float32,
        ),
        ("dp", "tensor"),
        scatter_dimension=0,
        tiled=True,
    )
    slice_width = slices.shape[0]
    returned = lax.all_to_all(
        slices.reshape(slice_width, experts, CAP), "expert", split_axis=1, concat_axis=1, tiled=True
    )
    returned = returned.reshape(slice_width, slot_count)
    token_grad = lax.dot_general(
        dispatch,
        returned,
        (((0,), (1,)), ((), ())),
        precision=lax.Precision.HIGHEST,
        preferred_element_type=jnp.float32,
    )
    input_grad = token_grad.astype(jnp.bfloat16)
    return (
        input_grad,
        grad_a.reshape(1, hidden_units, low_width),
        grad_b.reshape(1, low_width, col_width),
    )


MESH = pl.DeviceIdType.MESH
LANES = 128
F32 = jnp.float32
BF16 = jnp.bfloat16


def partner(index, step):
    bit = 1
    while bit <= step:
        if step & bit:
            index = index + bit - 2 * bit * lax.rem(lax.div(index, bit), 2)
        bit *= 2
    return index


def tdot(a, b):
    return lax.dot_general(a, b, (((0,), (0,)), ((), ())), preferred_element_type=F32)


def ndot(a, b):
    return lax.dot_general(a, b, (((1,), (1,)), ((), ())), preferred_element_type=F32)


def layer_kernel(
    sizes,
    tok_hbm, cot_hbm, ids_hbm, prob_hbm, ten_hbm, wg_ref, wu_ref, wd_ref, ain_ref, aout_ref,
    dx_hbm, ga_hbm, gb_hbm,
    dx_ref, ga_ref, gb_ref, tok_ref, cot_ref, ids_ref, prob_ref, ten_ref, rows, send, wgu, wgb, wda, ain, gu_mine, gu_theirs, bl_mine, bl_theirs, silu_keep, slope_keep, hid, grads, out_part, in_part, back_send, back, kept, low_mine, low_theirs,
    out_sem, in_sem, local_sem, w_send, w_recv, z_send, z_recv, p_send, p_recv, s_send, s_recv,
    r_send, r_recv, b_send, b_recv, l_send, l_recv,
):
    dp, ex, tn = sizes
    d, e, t = lax.axis_index("dp"), lax.axis_index("expert"), lax.axis_index("tensor")
    tokg, half = tok_hbm.shape
    wide = half // dp
    ff = wg_ref.shape[3]
    low = ain_ref.shape[2]
    hall = tn * ff
    slots = ex * CAP

    barrier = pltpu.get_barrier_semaphore()
    for axis, index, count in (("tensor", t, tn), ("dp", d, dp), ("expert", e, ex)):
        for step in range(1, count):
            pl.semaphore_signal(
                barrier, inc=1, device_id={axis: partner(index, step)}, device_id_type=MESH
            )

    loads = [
        pltpu.make_async_copy(s, o, in_sem.at[i])
        for i, (s, o) in enumerate(
            ((ids_hbm, ids_ref), (prob_hbm, prob_ref), (ten_hbm, ten_ref), (tok_hbm, tok_ref), (cot_hbm, cot_ref))
        )
    ]
    for c in loads:
        c.start()

    def remote(src, dst, ssem, rsem, axis, to):
        return pltpu.make_async_remote_copy(
            src_ref=src, dst_ref=dst, send_sem=ssem, recv_sem=rsem,
            device_id={axis: to}, device_id_type=MESH,
        )

    def lanes(start, size):
        return pl.ds(pl.multiple_of(start, LANES), size)

    def weight_parts(feat_owner, hid_owner):
        f = lanes(feat_owner * half, half)
        run = pl.ds(feat_owner * (dp // tn), dp // tn)
        gate_cols, up_cols = lanes(hid_owner * ff, ff), lanes(hall + hid_owner * ff, ff)
        return (
            (wg_ref.at[run], wgu.at[:, :, :, gate_cols]),
            (wu_ref.at[run], wgu.at[:, :, :, up_cols]),
            (wd_ref.at[0, :, f], wda.at[lanes(hid_owner * ff, ff), :]),
            (ain_ref.at[0], ain.at[lanes(hid_owner * ff, ff), :]),
            (wg_ref.at[:, feat_owner], wgb.at[:, :, gate_cols]),
            (wu_ref.at[:, feat_owner], wgb.at[:, :, up_cols]),
        )

    local = [
        pltpu.make_async_copy(s, o, local_sem.at[i])
        for i, (s, o) in enumerate(weight_parts(t, t))
    ]
    local.append(
        pltpu.make_async_copy(aout_ref.at[0, :, lanes(t * half, half)], wda.at[pl.ds(hall, low), :], local_sem.at[len(local)])
    )
    for c in local:
        c.start()

    for c in loads[:3]:
        c.wait()
    ti = lax.broadcasted_iota(jnp.int32, (tokg, tokg), 0)
    tj = lax.broadcasted_iota(jnp.int32, (tokg, tokg), 1)

    def column(row):
        wide_row = jnp.broadcast_to(row.astype(F32), (tokg, tokg))
        return jnp.sum(jnp.where(ti == tj, wide_row, 0.0), axis=1, keepdims=True)

    ids0, ids1 = column(ids_ref[0:1, :]).astype(jnp.int32), column(ids_ref[1:2, :]).astype(jnp.int32)
    probs = prob_ref[...].astype(F32)
    prob0, prob1 = column(probs[0:1, :]), column(probs[1:2, :])
    col = lax.broadcasted_iota(jnp.int32, (tokg, slots), 1)
    ecol = lax.div(col, CAP)
    scol = col - ecol * CAP
    hit0, hit1 = ids0 == ecol, ids1 == ecol
    named = jnp.where(hit0 | hit1, 1.0, 0.0)
    before = jnp.where(ti > tj, 1.0, 0.0).astype(BF16)
    place = jnp.dot(before, named.astype(BF16), preferred_element_type=F32)
    disp = jnp.where(place == scol.astype(F32), named, 0.0)
    disp = disp.astype(BF16)
    for c in loads[3:]:
        c.wait()
    mycols = lanes(d * wide, wide)
    send[:, :, 0:wide] = tdot(disp, tok_ref[:, mycols]).astype(BF16).reshape(ex, CAP, wide)

    pl.semaphore_wait(barrier, (tn - 1) + (dp - 1) + (ex - 1))

    sends = []
    z_parts = (pl.ds(0, wide), pl.ds(wide, wide + low))
    p_parts = (pl.ds(0, wide), pl.ds(wide, wide))

    def dispatch(i):
        for step in range(1, ex):
            to = partner(e, step)
            c = remote(
                send.at[to, :, z_parts[i]], rows.at[e, d, :, z_parts[i]],
                z_send.at[step, i], z_recv.at[e, i], "expert", to,
            )
            c.start()
            sends.append(c)

    dispatch(0)
    send[:, :, wide:2 * wide] = tdot(disp, cot_ref[:, mycols]).astype(BF16).reshape(ex, CAP, wide)
    weight = jnp.where(hit0, prob0, 0.0) + jnp.where(hit1, prob1, 0.0)
    tcol = column(ten_ref[...])
    lowcol = lax.div(lax.broadcasted_iota(jnp.int32, (tokg, low), 1), RANK).astype(F32)
    tmark = jnp.where(tcol == lowcol, 1.0, 0.0).astype(BF16)
    marked = jnp.where(disp > 0, weight, 0.0).astype(BF16)
    send[:, :, 2 * wide:] = tdot(marked, tmark).astype(BF16).reshape(ex, CAP, low)
    dispatch(1)
    for step in range(1, tn):
        to = partner(t, step)
        for i, (s, o) in enumerate(weight_parts(to, t)):
            c = remote(s, o, w_send.at[step, i], w_recv.at[t, i], "tensor", to)
            c.start()
            sends.append(c)

    def weights_here(i):
        local[i].wait()
        for step in range(1, tn):
            frm = partner(t, step)
            s, o = weight_parts(t, frm)[i]
            remote(s, o, w_send.at[step, i], w_recv.at[frm, i], "tensor", frm).wait_recv()

    scol_own = lax.broadcasted_iota(jnp.int32, (tokg, CAP), 1).astype(F32)
    named_own = jnp.where((ids0 == e) | (ids1 == e), 1.0, 0.0)
    named_own = jnp.broadcast_to(named_own, (tokg, CAP))
    place_own = jnp.dot(before, named_own.astype(BF16), preferred_element_type=F32)
    disp_own = jnp.where(place_own == scol_own, named_own, 0.0).astype(BF16)
    for k in range(dp):
        cols = slice(k * wide, (k + 1) * wide)
        rows[e, k, :, 0:wide] = tdot(disp_own, tok_ref[:, cols]).astype(BF16)
        rows[e, k, :, wide:2 * wide] = tdot(disp_own, cot_ref[:, cols]).astype(BF16)
    rows[e, d, :, 2 * wide:] = send[e, :, 2 * wide:]

    def pass_on(i):
        for step in range(1, ex):
            g = partner(e, step)
            part = rows.at[g, d, :, z_parts[i]]
            remote(part, part, z_send.at[step, i], z_recv.at[g, i], "expert", g).wait_recv()
            for hop in range(1, dp):
                part = rows.at[g, d, :, p_parts[i]]
                c = remote(part, part, p_send.at[step, hop, i], p_recv.at[g, d, i], "dp", partner(d, hop))
                c.start()
                sends.append(c)

    def gathered(i, hop):
        frm = partner(d, hop)
        if hop:
            for step in range(1, ex):
                g = partner(e, step)
                part = rows.at[g, frm, :, p_parts[i]]
                remote(part, part, p_send.at[step, hop, i], p_recv.at[g, frm, i], "dp", frm).wait_recv()
        return frm, rows[:, frm, :, i * wide:(i + 1) * wide].reshape(slots, wide)

    def exchange(i, acc, own, others):
        own[...] = acc
        copies = [
            remote(own, others.at[t], s_send.at[hop, i], s_recv.at[t, i], "tensor", partner(t, hop))
            for hop in range(1, tn)
        ]
        for c in copies:
            c.start()
        sends.extend(copies)

    def exchanged(i, own, others):
        total = own[...]
        for hop in range(1, tn):
            frm = partner(t, hop)
            remote(own, others.at[frm], s_send.at[hop, i], s_recv.at[frm, i], "tensor", frm).wait_recv()
            total = total + others[frm]
        return total

    pass_on(0)
    weights_here(0)
    weights_here(1)
    acc = jnp.zeros((slots, 2 * hall), F32)
    for hop in range(dp):
        k, x = gathered(0, hop)
        acc = acc + jnp.dot(x, wgu[lax.div(k, tn), lax.rem(k, tn)], preferred_element_type=F32)
    exchange(0, acc, gu_mine, gu_theirs)
    pass_on(1)
    weights_here(2)
    weights_here(3)
    local[6].wait()
    flags = rows[:, d, :, 2 * wide:].reshape(slots, low).astype(F32)
    row_weight = jnp.max(flags, axis=1, keepdims=True)
    flags = adapter_scale_factor * flags
    total = exchanged(0, gu_mine, gu_theirs)
    gate, up = total[:, 0:hall], total[:, hall:]
    sig = jax.nn.sigmoid(gate)
    silu = gate * sig
    hidden = (silu * up).astype(BF16)
    hid[...] = hidden
    a_in = ain[...]
    low_part = jnp.dot(hidden, a_in, preferred_element_type=F32)
    low_mine[...] = low_part.astype(BF16)
    silu_keep[...] = silu
    slope_keep[...] = up * (sig * (1.0 + gate * (1.0 - sig)))

    acc = jnp.zeros((slots, hall + low), F32)
    for hop in range(dp):
        k, y = gathered(1, hop)
        acc = acc + ndot(y, wda[:, lanes(k * wide, wide)])
    exchange(1, acc, bl_mine, bl_theirs)
    weights_here(4)
    weights_here(5)
    total = exchanged(1, bl_mine, bl_theirs)
    back_acc, low_acc = total[:, 0:hall], total[:, hall:]
    down_coef = (flags * low_acc).astype(BF16)
    hidden_grad = row_weight * back_acc + ndot(down_coef, a_in)
    grads[:, 0:hall] = (hidden_grad * slope_keep[...]).astype(BF16)
    grads[:, hall:] = (hidden_grad * silu_keep[...]).astype(BF16)

    def slice_grad(k):
        return ndot(grads[...], wgb[k])

    for hop in range(dp - 1, 0, -1):
        to = partner(d, hop)
        out_part[hop] = slice_grad(to).astype(BF16).reshape(ex, CAP, wide)
        for step in range(ex - 1, -1, -1):
            g = partner(e, step)
            c = remote(out_part.at[hop, g], in_part.at[d, g], r_send.at[hop, step], r_recv.at[d, g], "dp", to)
            c.start()
            sends.append(c)
    own = slice_grad(d).reshape(ex, CAP, wide)
    for hop in range(1, dp):
        c = remote(low_mine, low_theirs.at[d], l_send.at[hop], l_recv.at[d], "dp", partner(d, hop))
        c.start()
        sends.append(c)
    kept[...] = own
    ga_ref[...] = tdot(hid[:, lanes(t * ff, ff)], down_coef)
    results = [
        pltpu.make_async_copy(s, o, out_sem.at[i])
        for i, (s, o) in enumerate(((dx_ref, dx_hbm), (ga_ref, ga_hbm.at[0]), (gb_ref, gb_hbm.at[0])))
    ]
    results[1].start()

    for step in range(ex - 1, -1, -1):
        g = partner(e, step)
        acc = kept[g]
        for hop in range(dp - 1, 0, -1):
            frm = partner(d, hop)
            remote(out_part.at[hop, g], in_part.at[frm, g], r_send.at[hop, step], r_recv.at[frm, g], "dp", frm).wait_recv()
            acc = acc + in_part[frm, g].astype(F32)
        if step:
            back_send[step] = acc.astype(BF16)
            c = remote(back_send.at[step], back.at[e], b_send.at[step], b_recv.at[e], "expert", g)
            c.start()
            sends.append(c)
        else:
            back[e] = acc.astype(BF16)

    low_in = low_part
    for hop in range(1, dp):
        frm = partner(d, hop)
        remote(low_mine, low_theirs.at[frm], l_send.at[hop], l_recv.at[frm], "dp", frm).wait_recv()
    low_in = low_in + sum(low_theirs[partner(d, hop)].astype(F32) for hop in range(1, dp))
    up_coef = (flags * low_in).astype(BF16)
    for k in range(dp):
        y = rows[:, k, :, wide:2 * wide].reshape(slots, wide)
        gb_ref[:, k * wide:(k + 1) * wide] = tdot(up_coef, y)
    results[2].start()

    for step in range(1, ex):
        g = partner(e, step)
        remote(back_send.at[step], back.at[g], b_send.at[step], b_recv.at[g], "expert", g).wait_recv()
    dx_ref[...] = jnp.dot(disp, back[...].reshape(slots, wide), preferred_element_type=F32).astype(BF16)
    results[0].start()
    for c in sends:
        c.wait_send()
    for c in results:
        c.wait()


def write_kernel(a_ref, b_ref, c_ref, a_out, b_out, c_out, a_mid, b_mid, c_mid, in_sem, out_sem):
    halves = c_ref.shape[1] // 2
    first, second = pl.ds(0, halves), pl.ds(halves, halves)
    routes = (
        (c_ref.at[:, first], c_mid.at[:, first], c_out.at[:, first]),
        (c_ref.at[:, second], c_mid.at[:, second], c_out.at[:, second]),
        (b_ref, b_mid, b_out),
        (a_ref, a_mid, a_out),
    )
    loads = [pltpu.make_async_copy(s, m, in_sem.at[i]) for i, (s, m, _) in enumerate(routes)]
    stores = [pltpu.make_async_copy(m, o, out_sem.at[i]) for i, (_, m, o) in enumerate(routes)]
    for c in loads:
        c.start()
    for load, store in zip(loads, stores):
        load.wait()
        store.start()
    for c in stores:
        c.wait()


def fused(sizes, tokens, cotangent, expert_ids, gate_probs, tenant_ids, w_gate, w_up, w_down, adapter_in, adapter_out):
    dp, ex, tn = sizes
    tokg, half = tokens.shape
    wide = half // dp
    ff = w_gate.shape[2]
    low = adapter_in.shape[2]
    hall, slots = tn * ff, ex * CAP
    hbm = pl.BlockSpec(memory_space=pltpu.HBM)
    dma = pltpu.SemaphoreType.DMA
    shapes = (
        jax.ShapeDtypeStruct((tokg, wide), BF16),
        jax.ShapeDtypeStruct((1, ff, low), F32),
        jax.ShapeDtypeStruct((1, low, half), F32),
    )
    results = pl.pallas_call(
        functools.partial(layer_kernel, sizes),
        out_shape=shapes,
        in_specs=[hbm] * 10,
        out_specs=(hbm, hbm, hbm),
        scratch_shapes=[
            pltpu.VMEM((tokg, wide), BF16),
            pltpu.VMEM((ff, low), F32),
            pltpu.VMEM((low, half), F32),
            pltpu.VMEM((tokg, half), BF16),
            pltpu.VMEM((tokg, half), BF16),
            pltpu.VMEM((TOP, tokg), jnp.int32),
            pltpu.VMEM((TOP, tokg), BF16),
            pltpu.VMEM((1, tokg), jnp.int32),
            pltpu.VMEM((ex, dp, CAP, 2 * wide + low), BF16),
            pltpu.VMEM((ex, CAP, 2 * wide + low), BF16),
            pltpu.VMEM((dp // tn, tn, wide, 2 * hall), BF16),
            pltpu.VMEM((dp, wide, 2 * hall), BF16),
            pltpu.VMEM((hall + low, half), BF16),
            pltpu.VMEM((hall, low), BF16),
            pltpu.VMEM((slots, 2 * hall), F32),
            pltpu.VMEM((tn, slots, 2 * hall), F32),
            pltpu.VMEM((slots, hall + low), F32),
            pltpu.VMEM((tn, slots, hall + low), F32),
            pltpu.VMEM((slots, hall), F32),
            pltpu.VMEM((slots, hall), F32),
            pltpu.VMEM((slots, hall), BF16),
            pltpu.VMEM((slots, 2 * hall), BF16),
            pltpu.VMEM((dp, ex, CAP, wide), BF16),
            pltpu.VMEM((dp, ex, CAP, wide), BF16),
            pltpu.VMEM((ex, CAP, wide), BF16),
            pltpu.VMEM((ex, CAP, wide), BF16),
            pltpu.VMEM((ex, CAP, wide), F32),
            pltpu.VMEM((slots, low), BF16),
            pltpu.VMEM((dp, slots, low), BF16),
            dma((3,)), dma((5,)),
            dma((7,)),
            dma((tn, 6)), dma((tn, 6)),
            dma((ex, 2)), dma((ex, 2)),
            dma((ex, dp, 2)), dma((ex, dp, 2)),
            dma((tn, 2)), dma((tn, 2)),
            dma((dp, ex)), dma((dp, ex)),
            dma((ex,)), dma((ex,)),
            dma((dp,)), dma((dp,)),
        ],
        compiler_params=pltpu.CompilerParams(
            collective_id=0, has_side_effects=True, vmem_limit_bytes=62 * 1024 * 1024
        ),
        cost_estimate=pl.CostEstimate(flops=10**9, bytes_accessed=8 * 10**6, transcendentals=10**5),
    )(tokens, cotangent, expert_ids.T, gate_probs.T, tenant_ids.reshape(1, -1), w_gate.reshape(dp, tn, wide, ff), w_up.reshape(dp, tn, wide, ff), w_down, adapter_in, adapter_out)
    return pl.pallas_call(
        write_kernel,
        out_shape=shapes,
        in_specs=[hbm] * 3,
        out_specs=(hbm,) * 3,
        scratch_shapes=[pltpu.VMEM(r.shape, r.dtype) for r in results] + [dma((4,)), dma((4,))],
        compiler_params=pltpu.CompilerParams(vmem_limit_bytes=62 * 1024 * 1024),
    )(*results)


def body_for(mesh):
    sizes = (mesh.shape["dp"], mesh.shape["expert"], mesh.shape["tensor"])
    paired = all(n & (n - 1) == 0 for n in sizes)

    def body(tokens, *rest):
        if paired and sizes[0] % sizes[2] == 0 and tokens.shape[1] % (sizes[0] * LANES) == 0:
            return fused(sizes, tokens, *rest)
        return on_device(tokens, *rest)

    return body


def solution(mesh):
    placed = (
        P("expert", "tensor"),
        P("expert", "tensor"),
        P("expert", None),
        P("expert", None),
        P("expert"),
        P("expert", None, ("dp", "tensor")),
        P("expert", None, ("dp", "tensor")),
        P("expert", ("dp", "tensor"), None),
        P("expert", ("dp", "tensor"), None),
        P("expert", None, None),
    )
    return jax.shard_map(
        body_for(mesh),
        mesh=mesh,
        in_specs=placed,
        out_specs=(
            P("expert", ("dp", "tensor")),
            P("expert", ("dp", "tensor"), None),
            P("expert", None, "tensor"),
        ),
        check_vma=False,
    )
```

```python
import functools

import jax
import jax.numpy as jnp
from jax import lax
from jax.experimental import pallas as pl
from jax.experimental.pallas import tpu as pltpu
from jax.sharding import PartitionSpec as P

TEN = 8
RANK = 16
TOP = 2
CAP = 32


adapter_scale_factor = 2.0


def on_device(
    tokens,
    cotangent,
    expert_ids,
    gate_probs,
    tenant_ids,
    w_gate,
    w_up,
    w_down,
    adapter_in,
    adapter_out,
):
    experts = lax.axis_size("expert")
    tok_rows = tokens.shape[0]
    col_width = tokens.shape[1]
    slot_count = experts * CAP
    route_ids = expert_ids.reshape(-1)
    route_total = route_ids.shape[0]
    onehot = (route_ids[:, None] == jnp.arange(experts, dtype=jnp.int32)[None, :]).astype(jnp.int32)
    earlier = jnp.cumsum(onehot, axis=0) - onehot
    slot_index = jnp.sum(earlier * onehot, axis=1)
    target = route_ids * CAP + slot_index
    owner_token = jnp.arange(route_total, dtype=jnp.int32) // TOP
    slot_hits = (target[None, :] == jnp.arange(slot_count, dtype=jnp.int32)[:, None]).astype(
        jnp.float32
    )
    token_hits = (owner_token[:, None] == jnp.arange(tok_rows, dtype=jnp.int32)[None, :]).astype(
        jnp.float32
    )
    dispatch = jnp.dot(slot_hits, token_hits, precision=lax.Precision.HIGHEST)
    tenant_hot = (tenant_ids[:, None] == jnp.arange(TEN, dtype=jnp.int32)[None, :]).astype(
        jnp.float32
    )
    route_weight = gate_probs.reshape(-1).astype(jnp.float32)
    route_marks = (
        jnp.dot(token_hits, tenant_hot, precision=lax.Precision.HIGHEST) * route_weight[:, None]
    )
    slot_marks = jnp.dot(slot_hits, route_marks, precision=lax.Precision.HIGHEST)
    dispatch_half = dispatch.astype(jnp.bfloat16)
    send_inputs = jnp.dot(dispatch_half, tokens, preferred_element_type=jnp.float32).astype(
        jnp.bfloat16
    )
    send_grads = jnp.dot(dispatch_half, cotangent, preferred_element_type=jnp.float32).astype(
        jnp.bfloat16
    )
    send_inputs = send_inputs.reshape(experts, CAP, col_width)
    send_grads = send_grads.reshape(experts, CAP, col_width)
    send_marks = slot_marks.astype(jnp.bfloat16).reshape(experts, CAP, TEN)
    recv_inputs, recv_grads, recv_marks = (
        lax.all_to_all(send_inputs, "expert", split_axis=0, concat_axis=0, tiled=True),
        lax.all_to_all(send_grads, "expert", split_axis=0, concat_axis=0, tiled=True),
        lax.all_to_all(send_marks, "expert", split_axis=0, concat_axis=0, tiled=True),
    )
    gate_mat = w_gate[0]
    up_mat = w_up[0]
    down_mat = w_down[0]
    first_factor = adapter_in[0]
    second_factor = adapter_out[0]
    hidden_units = gate_mat.shape[1]
    low_width = first_factor.shape[1]
    input_piece = lax.all_gather(recv_inputs, "tensor", axis=2, tiled=True)
    grad_piece = lax.all_gather(recv_grads, "tensor", axis=2, tiled=True)
    piece_width = input_piece.shape[2]
    input_piece = input_piece.reshape(slot_count, piece_width)
    grad_piece = grad_piece.reshape(slot_count, piece_width)
    gate_rows = gate_mat
    up_projection_rows = up_mat
    gate_acc = jnp.dot(input_piece, gate_rows, preferred_element_type=jnp.float32)
    up_acc = jnp.dot(input_piece, up_projection_rows, preferred_element_type=jnp.float32)
    back_acc = lax.dot_general(
        grad_piece, down_mat, (((1,), (1,)), ((), ())), preferred_element_type=jnp.float32
    )
    low_acc = lax.dot_general(
        grad_piece, second_factor, (((1,), (1,)), ((), ())), preferred_element_type=jnp.float32
    )
    sig = jax.nn.sigmoid(gate_acc)
    silu_val = gate_acc * sig
    hidden = (silu_val * up_acc).astype(jnp.bfloat16)
    low_part = jnp.dot(hidden, first_factor, preferred_element_type=jnp.float32)
    marks_value = recv_marks.reshape(slot_count, TEN).astype(jnp.float32)
    row_weight = jnp.sum(marks_value, axis=1)
    broadcast_routing_flags = jnp.repeat(marks_value, RANK, axis=1)
    low_in = lax.psum(low_part, ("dp", "tensor"))
    gate_weighted_rows = adapter_scale_factor * broadcast_routing_flags
    down_coef = (gate_weighted_rows * low_acc).astype(jnp.bfloat16)
    up_coef = (gate_weighted_rows * low_in).astype(jnp.bfloat16)
    hidden_gradient = row_weight[:, None] * back_acc + lax.dot_general(
        down_coef, first_factor, (((1,), (1,)), ((), ())), preferred_element_type=jnp.float32
    )
    slope = sig * (1.0 + gate_acc * (1.0 - sig))
    gate_grad = (hidden_gradient * up_acc * slope).astype(jnp.bfloat16)
    up_grad = (hidden_gradient * silu_val).astype(jnp.bfloat16)
    grad_a = lax.dot_general(
        hidden, down_coef, (((0,), (0,)), ((), ())), preferred_element_type=jnp.float32
    )
    local_grads = recv_grads.reshape(slot_count, col_width)
    grad_b = lax.dot_general(
        up_coef, local_grads, (((0,), (0,)), ((), ())), preferred_element_type=jnp.float32
    )
    gate_rows = gate_mat
    up_projection_rows = up_mat
    term = lax.dot_general(
        gate_rows, gate_grad, (((1,), (1,)), ((), ())), preferred_element_type=jnp.float32
    )
    slices = lax.psum_scatter(
        term
        + lax.dot_general(
            up_projection_rows,
            up_grad,
            (((1,), (1,)), ((), ())),
            preferred_element_type=jnp.float32,
        ),
        ("dp", "tensor"),
        scatter_dimension=0,
        tiled=True,
    )
    slice_width = slices.shape[0]
    returned = lax.all_to_all(
        slices.reshape(slice_width, experts, CAP), "expert", split_axis=1, concat_axis=1, tiled=True
    )
    returned = returned.reshape(slice_width, slot_count)
    token_grad = lax.dot_general(
        dispatch,
        returned,
        (((0,), (1,)), ((), ())),
        precision=lax.Precision.HIGHEST,
        preferred_element_type=jnp.float32,
    )
    input_grad = token_grad.astype(jnp.bfloat16)
    return (
        input_grad,
        grad_a.reshape(1, hidden_units, low_width),
        grad_b.reshape(1, low_width, col_width),
    )


MESH = pl.DeviceIdType.MESH
LANES = 128
F32 = jnp.float32
BF16 = jnp.bfloat16


def partner(index, step):
    bit = 1
    while bit <= step:
        if step & bit:
            index = index + bit - 2 * bit * lax.rem(lax.div(index, bit), 2)
        bit *= 2
    return index


def tdot(a, b):
    return lax.dot_general(a, b, (((0,), (0,)), ((), ())), preferred_element_type=F32)


def ndot(a, b):
    return lax.dot_general(a, b, (((1,), (1,)), ((), ())), preferred_element_type=F32)


def layer_kernel(
    sizes,
    tok_hbm, cot_hbm, ids_hbm, prob_hbm, ten_hbm, wg_ref, wu_ref, wd_ref, ain_ref, aout_ref,
    dx_hbm, ga_hbm, gb_hbm,
    dx_ref, ga_ref, gb_ref, tok_ref, cot_ref, ids_ref, prob_ref, ten_ref, rows, send, wgu, wgb, wda, ain, gu_mine, gu_theirs, bl_mine, bl_theirs, silu_keep, slope_keep, hid, grads, out_part, in_part, back_send, back, kept, low_mine, low_theirs,
    out_sem, in_sem, local_sem, w_send, w_recv, z_send, z_recv, p_send, p_recv, s_send, s_recv,
    r_send, r_recv, b_send, b_recv, l_send, l_recv,
):
    dp, ex, tn = sizes
    d, e, t = lax.axis_index("dp"), lax.axis_index("expert"), lax.axis_index("tensor")
    tokg, half = tok_hbm.shape
    wide = half // dp
    ff = wg_ref.shape[3]
    low = ain_ref.shape[2]
    hall = tn * ff
    slots = ex * CAP

    barrier = pltpu.get_barrier_semaphore()
    for axis, index, count in (("tensor", t, tn), ("dp", d, dp), ("expert", e, ex)):
        for step in range(1, count):
            pl.semaphore_signal(
                barrier, inc=1, device_id={axis: partner(index, step)}, device_id_type=MESH
            )

    loads = [
        pltpu.make_async_copy(s, o, in_sem.at[i])
        for i, (s, o) in enumerate(
            ((ids_hbm, ids_ref), (prob_hbm, prob_ref), (ten_hbm, ten_ref), (tok_hbm, tok_ref), (cot_hbm, cot_ref))
        )
    ]
    for c in loads:
        c.start()

    def remote(src, dst, ssem, rsem, axis, to):
        return pltpu.make_async_remote_copy(
            src_ref=src, dst_ref=dst, send_sem=ssem, recv_sem=rsem,
            device_id={axis: to}, device_id_type=MESH,
        )

    def lanes(start, size):
        return pl.ds(pl.multiple_of(start, LANES), size)

    def weight_parts(feat_owner, hid_owner):
        f = lanes(feat_owner * half, half)
        run = pl.ds(feat_owner * (dp // tn), dp // tn)
        gate_cols, up_cols = lanes(hid_owner * ff, ff), lanes(hall + hid_owner * ff, ff)
        return (
            (wg_ref.at[run], wgu.at[:, :, :, gate_cols]),
            (wu_ref.at[run], wgu.at[:, :, :, up_cols]),
            (wd_ref.at[0, :, f], wda.at[lanes(hid_owner * ff, ff), :]),
            (ain_ref.at[0], ain.at[lanes(hid_owner * ff, ff), :]),
            (wg_ref.at[:, feat_owner], wgb.at[:, :, gate_cols]),
            (wu_ref.at[:, feat_owner], wgb.at[:, :, up_cols]),
        )

    local = [
        pltpu.make_async_copy(s, o, local_sem.at[i])
        for i, (s, o) in enumerate(weight_parts(t, t))
    ]
    local.append(
        pltpu.make_async_copy(aout_ref.at[0, :, lanes(t * half, half)], wda.at[pl.ds(hall, low), :], local_sem.at[len(local)])
    )
    for c in local:
        c.start()

    for c in loads[:3]:
        c.wait()
    ti = lax.broadcasted_iota(jnp.int32, (tokg, tokg), 0)
    tj = lax.broadcasted_iota(jnp.int32, (tokg, tokg), 1)

    def column(row):
        wide_row = jnp.broadcast_to(row.astype(F32), (tokg, tokg))
        return jnp.sum(jnp.where(ti == tj, wide_row, 0.0), axis=1, keepdims=True)

    ids0, ids1 = column(ids_ref[0:1, :]).astype(jnp.int32), column(ids_ref[1:2, :]).astype(jnp.int32)
    probs = prob_ref[...].astype(F32)
    prob0, prob1 = column(probs[0:1, :]), column(probs[1:2, :])
    col = lax.broadcasted_iota(jnp.int32, (tokg, slots), 1)
    ecol = lax.div(col, CAP)
    scol = col - ecol * CAP
    hit0, hit1 = ids0 == ecol, ids1 == ecol
    named = jnp.where(hit0 | hit1, 1.0, 0.0)
    before = jnp.where(ti > tj, 1.0, 0.0).astype(BF16)
    place = jnp.dot(before, named.astype(BF16), preferred_element_type=F32)
    disp = jnp.where(place == scol.astype(F32), named, 0.0)
    disp = disp.astype(BF16)
    for c in loads[3:]:
        c.wait()
    mycols = lanes(d * wide, wide)
    send[:, :, 0:wide] = tdot(disp, tok_ref[:, mycols]).astype(BF16).reshape(ex, CAP, wide)

    pl.semaphore_wait(barrier, (tn - 1) + (dp - 1) + (ex - 1))

    sends = []
    z_parts = (pl.ds(0, wide), pl.ds(wide, wide + low))
    p_parts = (pl.ds(0, wide), pl.ds(wide, wide))

    def dispatch(i):
        for step in range(1, ex):
            to = partner(e, step)
            c = remote(
                send.at[to, :, z_parts[i]], rows.at[e, d, :, z_parts[i]],
                z_send.at[step, i], z_recv.at[e, i], "expert", to,
            )
            c.start()
            sends.append(c)

    dispatch(0)
    send[:, :, wide:2 * wide] = tdot(disp, cot_ref[:, mycols]).astype(BF16).reshape(ex, CAP, wide)
    weight = jnp.where(hit0, prob0, 0.0) + jnp.where(hit1, prob1, 0.0)
    tcol = column(ten_ref[...])
    lowcol = lax.div(lax.broadcasted_iota(jnp.int32, (tokg, low), 1), RANK).astype(F32)
    tmark = jnp.where(tcol == lowcol, 1.0, 0.0).astype(BF16)
    marked = jnp.where(disp > 0, weight, 0.0).astype(BF16)
    send[:, :, 2 * wide:] = tdot(marked, tmark).astype(BF16).reshape(ex, CAP, low)
    dispatch(1)
    for step in range(1, tn):
        to = partner(t, step)
        for i, (s, o) in enumerate(weight_parts(to, t)):
            c = remote(s, o, w_send.at[step, i], w_recv.at[t, i], "tensor", to)
            c.start()
            sends.append(c)

    def weights_here(i):
        local[i].wait()
        for step in range(1, tn):
            frm = partner(t, step)
            s, o = weight_parts(t, frm)[i]
            remote(s, o, w_send.at[step, i], w_recv.at[frm, i], "tensor", frm).wait_recv()

    scol_own = lax.broadcasted_iota(jnp.int32, (tokg, CAP), 1).astype(F32)
    named_own = jnp.where((ids0 == e) | (ids1 == e), 1.0, 0.0)
    named_own = jnp.broadcast_to(named_own, (tokg, CAP))
    place_own = jnp.dot(before, named_own.astype(BF16), preferred_element_type=F32)
    disp_own = jnp.where(place_own == scol_own, named_own, 0.0).astype(BF16)
    for k in range(dp):
        cols = slice(k * wide, (k + 1) * wide)
        rows[e, k, :, 0:wide] = tdot(disp_own, tok_ref[:, cols]).astype(BF16)
        rows[e, k, :, wide:2 * wide] = tdot(disp_own, cot_ref[:, cols]).astype(BF16)
    rows[e, d, :, 2 * wide:] = send[e, :, 2 * wide:]

    def pass_on(i):
        for step in range(1, ex):
            g = partner(e, step)
            part = rows.at[g, d, :, z_parts[i]]
            remote(part, part, z_send.at[step, i], z_recv.at[g, i], "expert", g).wait_recv()
            for hop in range(1, dp):
                part = rows.at[g, d, :, p_parts[i]]
                c = remote(part, part, p_send.at[step, hop, i], p_recv.at[g, d, i], "dp", partner(d, hop))
                c.start()
                sends.append(c)

    def gathered(i, hop):
        frm = partner(d, hop)
        if hop:
            for step in range(1, ex):
                g = partner(e, step)
                part = rows.at[g, frm, :, p_parts[i]]
                remote(part, part, p_send.at[step, hop, i], p_recv.at[g, frm, i], "dp", frm).wait_recv()
        return frm, rows[:, frm, :, i * wide:(i + 1) * wide].reshape(slots, wide)

    def exchange(i, acc, own, others):
        own[...] = acc
        copies = [
            remote(own, others.at[t], s_send.at[hop, i], s_recv.at[t, i], "tensor", partner(t, hop))
            for hop in range(1, tn)
        ]
        for c in copies:
            c.start()
        sends.extend(copies)

    def exchanged(i, own, others):
        total = own[...]
        for hop in range(1, tn):
            frm = partner(t, hop)
            remote(own, others.at[frm], s_send.at[hop, i], s_recv.at[frm, i], "tensor", frm).wait_recv()
            total = total + others[frm]
        return total

    pass_on(0)
    pass_on(1)
    weights_here(0)
    weights_here(1)
    acc = jnp.zeros((slots, 2 * hall), F32)
    for hop in range(dp):
        k, x = gathered(0, hop)
        acc = acc + jnp.dot(x, wgu[lax.div(k, tn), lax.rem(k, tn)], preferred_element_type=F32)
    exchange(0, acc, gu_mine, gu_theirs)
    weights_here(2)
    weights_here(3)
    local[6].wait()
    flags = rows[:, d, :, 2 * wide:].reshape(slots, low).astype(F32)
    row_weight = jnp.max(flags, axis=1, keepdims=True)
    flags = adapter_scale_factor * flags
    total = exchanged(0, gu_mine, gu_theirs)
    gate, up = total[:, 0:hall], total[:, hall:]
    sig = jax.nn.sigmoid(gate)
    silu = gate * sig
    hidden = (silu * up).astype(BF16)
    hid[...] = hidden
    a_in = ain[...]
    low_part = jnp.dot(hidden, a_in, preferred_element_type=F32)
    low_mine[...] = low_part.astype(BF16)
    silu_keep[...] = silu
    slope_keep[...] = up * (sig * (1.0 + gate * (1.0 - sig)))

    acc = jnp.zeros((slots, hall + low), F32)
    for hop in range(dp):
        k, y = gathered(1, hop)
        acc = acc + ndot(y, wda[:, lanes(k * wide, wide)])
    exchange(1, acc, bl_mine, bl_theirs)
    weights_here(4)
    weights_here(5)
    total = exchanged(1, bl_mine, bl_theirs)
    back_acc, low_acc = total[:, 0:hall], total[:, hall:]
    down_coef = (flags * low_acc).astype(BF16)
    hidden_grad = row_weight * back_acc + ndot(down_coef, a_in)
    grads[:, 0:hall] = (hidden_grad * slope_keep[...]).astype(BF16)
    grads[:, hall:] = (hidden_grad * silu_keep[...]).astype(BF16)

    def slice_grad(k):
        return ndot(grads[...], wgb[k])

    for hop in range(dp - 1, 0, -1):
        to = partner(d, hop)
        out_part[hop] = slice_grad(to).astype(BF16).reshape(ex, CAP, wide)
        for step in range(ex - 1, -1, -1):
            g = partner(e, step)
            c = remote(out_part.at[hop, g], in_part.at[d, g], r_send.at[hop, step], r_recv.at[d, g], "dp", to)
            c.start()
            sends.append(c)
    own = slice_grad(d).reshape(ex, CAP, wide)
    for hop in range(1, dp):
        c = remote(low_mine, low_theirs.at[d], l_send.at[hop], l_recv.at[d], "dp", partner(d, hop))
        c.start()
        sends.append(c)
    kept[...] = own
    ga_ref[...] = tdot(hid[:, lanes(t * ff, ff)], down_coef)
    results = [
        pltpu.make_async_copy(s, o, out_sem.at[i])
        for i, (s, o) in enumerate(((dx_ref, dx_hbm), (ga_ref, ga_hbm.at[0]), (gb_ref, gb_hbm.at[0])))
    ]
    results[1].start()

    for step in range(ex - 1, -1, -1):
        g = partner(e, step)
        acc = kept[g]
        for hop in range(dp - 1, 0, -1):
            frm = partner(d, hop)
            remote(out_part.at[hop, g], in_part.at[frm, g], r_send.at[hop, step], r_recv.at[frm, g], "dp", frm).wait_recv()
            acc = acc + in_part[frm, g].astype(F32)
        if step:
            back_send[step] = acc.astype(BF16)
            c = remote(back_send.at[step], back.at[e], b_send.at[step], b_recv.at[e], "expert", g)
            c.start()
            sends.append(c)
        else:
            back[e] = acc.astype(BF16)

    low_in = low_part
    for hop in range(1, dp):
        frm = partner(d, hop)
        remote(low_mine, low_theirs.at[frm], l_send.at[hop], l_recv.at[frm], "dp", frm).wait_recv()
    low_in = low_in + sum(low_theirs[partner(d, hop)].astype(F32) for hop in range(1, dp))
    up_coef = (flags * low_in).astype(BF16)
    for k in range(dp):
        y = rows[:, k, :, wide:2 * wide].reshape(slots, wide)
        gb_ref[:, k * wide:(k + 1) * wide] = tdot(up_coef, y)
    results[2].start()

    for step in range(1, ex):
        g = partner(e, step)
        remote(back_send.at[step], back.at[g], b_send.at[step], b_recv.at[g], "expert", g).wait_recv()
    dx_ref[...] = jnp.dot(disp, back[...].reshape(slots, wide), preferred_element_type=F32).astype(BF16)
    results[0].start()
    for c in sends:
        c.wait_send()
    for c in results:
        c.wait()


def write_kernel(a_ref, b_ref, c_ref, a_out, b_out, c_out, a_mid, b_mid, c_mid, in_sem, out_sem):
    halves = c_ref.shape[1] // 2
    first, second = pl.ds(0, halves), pl.ds(halves, halves)
    routes = (
        (c_ref.at[:, first], c_mid.at[:, first], c_out.at[:, first]),
        (c_ref.at[:, second], c_mid.at[:, second], c_out.at[:, second]),
        (b_ref, b_mid, b_out),
        (a_ref, a_mid, a_out),
    )
    loads = [pltpu.make_async_copy(s, m, in_sem.at[i]) for i, (s, m, _) in enumerate(routes)]
    stores = [pltpu.make_async_copy(m, o, out_sem.at[i]) for i, (_, m, o) in enumerate(routes)]
    for c in loads:
        c.start()
    for load, store in zip(loads, stores):
        load.wait()
        store.start()
    for c in stores:
        c.wait()


def fused(sizes, tokens, cotangent, expert_ids, gate_probs, tenant_ids, w_gate, w_up, w_down, adapter_in, adapter_out):
    dp, ex, tn = sizes
    tokg, half = tokens.shape
    wide = half // dp
    ff = w_gate.shape[2]
    low = adapter_in.shape[2]
    hall, slots = tn * ff, ex * CAP
    hbm = pl.BlockSpec(memory_space=pltpu.HBM)
    dma = pltpu.SemaphoreType.DMA
    shapes = (
        jax.ShapeDtypeStruct((tokg, wide), BF16),
        jax.ShapeDtypeStruct((1, ff, low), F32),
        jax.ShapeDtypeStruct((1, low, half), F32),
    )
    results = pl.pallas_call(
        functools.partial(layer_kernel, sizes),
        out_shape=shapes,
        in_specs=[hbm] * 10,
        out_specs=(hbm, hbm, hbm),
        scratch_shapes=[
            pltpu.VMEM((tokg, wide), BF16),
            pltpu.VMEM((ff, low), F32),
            pltpu.VMEM((low, half), F32),
            pltpu.VMEM((tokg, half), BF16),
            pltpu.VMEM((tokg, half), BF16),
            pltpu.VMEM((TOP, tokg), jnp.int32),
            pltpu.VMEM((TOP, tokg), BF16),
            pltpu.VMEM((1, tokg), jnp.int32),
            pltpu.VMEM((ex, dp, CAP, 2 * wide + low), BF16),
            pltpu.VMEM((ex, CAP, 2 * wide + low), BF16),
            pltpu.VMEM((dp // tn, tn, wide, 2 * hall), BF16),
            pltpu.VMEM((dp, wide, 2 * hall), BF16),
            pltpu.VMEM((hall + low, half), BF16),
            pltpu.VMEM((hall, low), BF16),
            pltpu.VMEM((slots, 2 * hall), F32),
            pltpu.VMEM((tn, slots, 2 * hall), F32),
            pltpu.VMEM((slots, hall + low), F32),
            pltpu.VMEM((tn, slots, hall + low), F32),
            pltpu.VMEM((slots, hall), F32),
            pltpu.VMEM((slots, hall), F32),
            pltpu.VMEM((slots, hall), BF16),
            pltpu.VMEM((slots, 2 * hall), BF16),
            pltpu.VMEM((dp, ex, CAP, wide), BF16),
            pltpu.VMEM((dp, ex, CAP, wide), BF16),
            pltpu.VMEM((ex, CAP, wide), BF16),
            pltpu.VMEM((ex, CAP, wide), BF16),
            pltpu.VMEM((ex, CAP, wide), F32),
            pltpu.VMEM((slots, low), BF16),
            pltpu.VMEM((dp, slots, low), BF16),
            dma((3,)), dma((5,)),
            dma((7,)),
            dma((tn, 6)), dma((tn, 6)),
            dma((ex, 2)), dma((ex, 2)),
            dma((ex, dp, 2)), dma((ex, dp, 2)),
            dma((tn, 2)), dma((tn, 2)),
            dma((dp, ex)), dma((dp, ex)),
            dma((ex,)), dma((ex,)),
            dma((dp,)), dma((dp,)),
        ],
        compiler_params=pltpu.CompilerParams(
            collective_id=0, has_side_effects=True, vmem_limit_bytes=62 * 1024 * 1024
        ),
        cost_estimate=pl.CostEstimate(flops=10**9, bytes_accessed=8 * 10**6, transcendentals=10**5),
    )(tokens, cotangent, expert_ids.T, gate_probs.T, tenant_ids.reshape(1, -1), w_gate.reshape(dp, tn, wide, ff), w_up.reshape(dp, tn, wide, ff), w_down, adapter_in, adapter_out)
    return pl.pallas_call(
        write_kernel,
        out_shape=shapes,
        in_specs=[hbm] * 3,
        out_specs=(hbm,) * 3,
        scratch_shapes=[pltpu.VMEM(r.shape, r.dtype) for r in results] + [dma((4,)), dma((4,))],
        compiler_params=pltpu.CompilerParams(vmem_limit_bytes=62 * 1024 * 1024),
    )(*results)


def body_for(mesh):
    sizes = (mesh.shape["dp"], mesh.shape["expert"], mesh.shape["tensor"])
    paired = all(n & (n - 1) == 0 for n in sizes)

    def body(tokens, *rest):
        if paired and sizes[0] % sizes[2] == 0 and tokens.shape[1] % (sizes[0] * LANES) == 0:
            return fused(sizes, tokens, *rest)
        return on_device(tokens, *rest)

    return body


def solution(mesh):
    placed = (
        P("expert", "tensor"),
        P("expert", "tensor"),
        P("expert", None),
        P("expert", None),
        P("expert"),
        P("expert", None, ("dp", "tensor")),
        P("expert", None, ("dp", "tensor")),
        P("expert", ("dp", "tensor"), None),
        P("expert", ("dp", "tensor"), None),
        P("expert", None, None),
    )
    return jax.shard_map(
        body_for(mesh),
        mesh=mesh,
        in_specs=placed,
        out_specs=(
            P("expert", ("dp", "tensor")),
            P("expert", ("dp", "tensor"), None),
            P("expert", None, "tensor"),
        ),
        check_vma=False,
    )
```
